512 devices in a mesh: dp: 16 (over z), expert: 32 (over x, y, core).
Axes of the slice: x: 4, y: 4, z: 16, core: 2. Of those that a mesh axis runs over, the one named last changes fastest.
Arguments:
- tokens: bfloat16 [65536, 1024], P(('dp', 'expert')), may hold values from -6 to 6
- route_ids: int32 [65536, 4], P(('dp', 'expert')), may hold values from 0 to 31, all different within a row; in each aligned block of 128 rows (0 to 127, 128 to 255, ...) at most 24 rows name the same one
- route_weights: float32 [65536, 4], P(('dp', 'expert')), may hold values from 0.2 to 1
- up_weight: bfloat16 [32, 1024, 704], P('expert', 'dp'), may hold values from -0.1875 to 0.1875
- down_weight: bfloat16 [32, 1024, 704], P('expert', 'dp'), may hold values from -0.21875 to 0.21875
- head_weight: bfloat16 [1024, 1024], P('dp'), may hold values from -0.75 to 0.75
- out_weight: float32 [1024], P('dp'), may hold values from -0.375 to 0.375
- pool_ids: int32 [512, 128], P(('dp', 'expert')), may hold values from 0 to 15, never falling along the last dimension, each value on 1 to 64 neighbouring positions
- list_ids: int32 [512, 16], P(('dp', 'expert')), may hold values from 0 to 7, as said below
- clicks: int32 [512, 16], P(('dp', 'expert')), may hold values 0 or 1
- ranks: int32 [512, 16], P(('dp', 'expert')), may hold values from 0 to 31
- alpha_table: float32 [32], replicated, may hold values from 0.3 to 1
- beta_table: float32 [32], replicated, may hold values from 0 to 0.3
Outputs:
- grad_up: bfloat16 [32, 1024, 704], P('expert', 'dp')
- grad_down: bfloat16 [32, 1024, 704], P('expert', 'dp')
- grad_head: float32 [1024, 1024], P('dp')
- grad_out: float32 [1024], P('dp')
- list_loss: float32 [32], P('expert')
The draws below stay inside these ranges and needn't reach their ends.
Inputs may be any that keep to these rules, and one draw needn't show every extreme that they name: `route_ids`: each token names 4 different experts; among the 128 tokens of one device no expert is named more than 24 times, a bound that some block reaches. `pool_ids`: in each row the candidate number never falls, every candidate has 1 to 64 tokens and one has exactly 64. `list_ids`: every list number appears in every row.
All inputs are finite; a program needn't handle non-finite values. No bound on the sum of `clicks` on one device may be relied on, other than what follows from the above.
Results may differ from the reference program's by a relative error of at most 0.028.
Values may be sent and summed in bfloat16 or wider, within the bound.
A program may use at most 64 MiB of HBM per device.

```python
import math
import jax
import jax.numpy as jnp
import numpy as np
from jax import lax

D = 1024
FF = 704
HEAD = 1024
TOP = 4
TOK_DEV = 128
CAND_DEV = 16
SEG_MOST = 64
LISTS = 8
RANKS = 32
EXPERTS = 32
CAP = 24
TOKENS = 65536
SHARDS = 512
N_DP = 16
N_EXPERT = 32


def draw_list_ids(key, part):
    row_keys = jax.random.split(jax.random.fold_in(key, 11), SHARDS)
    permuted = jax.vmap(lambda single: jax.random.permutation(single, LISTS))(row_keys).astype(jnp.int32)
    filler = jax.random.randint(jax.random.fold_in(key, 12), (SHARDS, CAND_DEV), 0, LISTS).astype(jnp.int32)
    padded = jnp.concatenate([permuted, jnp.zeros((SHARDS, CAND_DEV - LISTS), jnp.int32)], axis=1)
    columns = jnp.arange(CAND_DEV, dtype=jnp.int32)[None, :]
    return jnp.where(columns < LISTS, padded, filler).astype(jnp.int32)


def place_ends(drawn, rng, least, high):
    shape = drawn.shape
    spot = [jax.random.randint(jax.random.fold_in(rng, axis), (), 0, shape[axis]) for axis in range(len(shape))]
    drawn = drawn.at[tuple(spot)].set(least)
    longest = shape.index(max(shape))
    spot[longest] = (spot[longest] + 1) % shape[longest]
    return drawn.at[tuple(spot)].set(high)


def block_levels(rng, dims, cuts, smallest, largest):
    def one(dim, shards_of):
        draws = jax.random.uniform(jax.random.fold_in(jax.random.fold_in(rng, 6), dim), (shards_of,), jnp.float32, smallest / len(cuts), largest / len(cuts))
        return jnp.repeat(jnp.exp(draws), dims[dim] // shards_of).reshape((-1,) + (1,) * (len(dims) - dim - 1))

    level = one(*cuts[0])
    for cut in cuts[1:]:
        level = level * one(*cut)
    return level


def length_profile(amount, total, reach, skew):
    weights = [(1 << 20) // math.isqrt(standing ** skew) + 1 for standing in range(2, amount + 1)]
    surplus, counts = total - reach - (amount - 1), [1] * (amount - 1)
    while surplus > 0:
        free = [i for i in range(amount - 1) if counts[i] < reach]
        whole, remaining = sum([weights[i] for i in free]), surplus
        for i in free:
            extra = min(reach - counts[i], max(1, remaining * weights[i] // whole), surplus)
            counts[i] = counts[i] + extra
            surplus = surplus - extra
    return np.array([reach] + counts)


def ragged(stream_key, count, total, bound, skew):
    if count == 2:
        one = jax.random.randint(stream_key, (), max(1, total - bound), min(bound, total - 1) + 1)
        return jnp.stack([one, total - one])
    tallies = jnp.asarray(length_profile(count, total, bound, skew), jnp.int32)
    couples = (count - 1) // 2
    donor, receiver = tallies[1:1 + 2 * couples:2], tallies[2:2 + 2 * couples:2]
    slack = jnp.minimum(donor - 1, bound - receiver)
    passed = jax.random.randint(jax.random.fold_in(stream_key, 1), (couples,), 0, 1 << 20) % (slack + 1)
    tallies = tallies.at[1:1 + 2 * couples:2].set(donor - passed).at[2:2 + 2 * couples:2].set(receiver + passed)
    return tallies[jax.random.permutation(jax.random.fold_in(stream_key, 2), count)]


def deal_out(own_key, own, number, rows, number_of, top, bound, skew):
    sequence = jax.random.permutation(own_key, number_of)
    heavy_load, usual = load_shares(number_of, rows * top, bound, skew, True), load_shares(number_of, rows * top, bound, skew, False)
    places = jnp.arange(number_of)

    def named(tallies, offset_by):
        used = int((tallies > 0).sum())
        fixed = max(1, used // 4)
        shifted = fixed + (places - fixed + offset_by * (used - fixed)) % max(1, number_of - fixed)
        return jnp.zeros((number_of,), jnp.int32).at[sequence[jnp.where(places < fixed, places, shifted)]].set(jnp.asarray(tallies, jnp.int32))

    tallies = jnp.where(number % 4 == 0, named(heavy_load, number // 4), named(usual, number - number // 4 - 1))
    mixed = jax.random.permutation(jax.random.fold_in(own, 3), number_of)
    giver, receiver = mixed[0:number_of // 2 * 2:2], mixed[1:number_of // 2 * 2:2]
    margin = jnp.minimum(tallies[giver] - 1, bound - tallies[receiver]) // 2
    margin = jnp.where((giver == sequence[0]) | (receiver == sequence[0]) | (tallies[receiver] == 0), 0, jnp.maximum(margin, 0))
    shifted = jax.random.randint(jax.random.fold_in(own, 4), (number_of // 2,), 0, 1 << 20) % (margin + 1)
    tallies = tallies.at[giver].add(-shifted).at[receiver].add(shifted)
    labels = jnp.searchsorted(jnp.cumsum(tallies), jnp.arange(rows * top), side="right").astype(jnp.int32)
    table = labels.reshape(top, rows).T
    table = table[jax.random.permutation(jax.random.fold_in(own, 1), rows)]
    offset_by = jax.random.randint(jax.random.fold_in(own, 2), (rows, 1), 0, top)
    return jnp.take_along_axis(table, (jnp.arange(top)[None, :] + offset_by) % top, axis=1)


def load_shares(amount, total, limit, skew, full):
    loads = [(1 << 20) // math.isqrt(standing ** skew) + 1 for standing in range(1, amount + 1)]
    largest = limit if full else min(limit, max(-(-total // amount), total * loads[0] // sum(loads)))
    least = 1 if total - largest >= amount - 1 else 0
    given, spare = [largest] + [least] * (amount - 1), total - largest - least * (amount - 1)
    while spare > 0:
        free = [i for i in range(1, amount) if given[i] < largest] or [i for i in range(1, amount) if given[i] < limit]
        mass, left = sum([loads[i] for i in free]), spare
        for i in free:
            addition = min(limit - given[i], max(1, left * loads[i] // mass), spare)
            given[i] = given[i] + addition
            spare = spare - addition
    return np.array(given)


def noise(rng, extent, scale, limit, cuts=(), held_as=jnp.bfloat16):
    factor_of = block_levels(rng, extent, cuts, -0.22, 0.18) if cuts else 1.0
    entries = jax.random.normal(rng, extent, jnp.float32) * scale * factor_of
    return jnp.minimum(jnp.maximum(entries, -limit), limit).astype(held_as)


def setup_inputs(seed: int = 0) -> dict:
    key_of = jax.random.split(jax.random.key(seed), 14)
    tokens = noise(key_of[0], (TOKENS, D), 1.0, 6.0, ((0, 512),))
    route_ids_keys = jax.random.split(jax.random.fold_in(key_of[1], 1), TOKENS // TOK_DEV)
    route_ids_turns = jax.random.permutation(jax.random.fold_in(key_of[1], 3), TOKENS // TOK_DEV)
    route_ids = jax.vmap(lambda own, number: deal_out(jax.random.fold_in(key_of[1], 2), own, number, TOK_DEV, EXPERTS, TOP, CAP, 2))(route_ids_keys, route_ids_turns).reshape((TOKENS, TOP))
    route_weights = jnp.clip(0.2 + 0.8 * jax.random.uniform(key_of[2], (TOKENS, TOP), jnp.float32) ** block_levels(key_of[2], (TOKENS, TOP), ((0, 512),), -0.2, 0.2), 0.2, 1.0)
    up_weight = noise(key_of[3], (EXPERTS, D, FF), D ** -0.5, 0.1875, ((0, 32), (1, 16)))
    down_weight = noise(key_of[4], (EXPERTS, D, FF), FF ** -0.5, 0.21875, ((0, 32), (1, 16)))
    head_weight = noise(key_of[5], (HEAD, D), (D // 16) ** -0.5, 0.75, ((0, 16),))
    out_weight = noise(key_of[6], (HEAD,), (HEAD // 4) ** -0.5, 0.375, ((0, 16),), jnp.float32)
    pool_ids = jax.vmap(lambda own: jnp.searchsorted(jnp.cumsum(ragged(own, CAND_DEV, TOK_DEV, SEG_MOST, 0)), jnp.arange(TOK_DEV), side="right"))(jax.random.split(key_of[7], SHARDS)).reshape((SHARDS, TOK_DEV)).astype(jnp.int32)
    list_ids = draw_list_ids(jax.random.fold_in(key_of[13], 71), 0)
    clicks = place_ends((jax.random.randint(key_of[9], (SHARDS, CAND_DEV), 0, 3) < 1).astype(jnp.int32), jax.random.fold_in(key_of[9], 1), 0, 1)
    ranks = place_ends(jax.random.randint(key_of[10], (SHARDS, CAND_DEV), 0, RANKS), jax.random.fold_in(key_of[10], 1), 0, RANKS - 1).astype(jnp.int32)
    alpha_table = jnp.clip(jnp.exp(jax.random.uniform(key_of[11], (RANKS,), jnp.float32, math.log(0.3), math.log(1.0))), 0.3, 1.0)
    beta_table = jnp.clip(jax.random.uniform(key_of[12], (RANKS,), jnp.float32, 0.0, 0.3), 0.0, 0.3)
    return dict(tokens=tokens, route_ids=route_ids, route_weights=route_weights, up_weight=up_weight, down_weight=down_weight, head_weight=head_weight, out_weight=out_weight, pool_ids=pool_ids, list_ids=list_ids, clicks=clicks, ranks=ranks, alpha_table=alpha_table, beta_table=beta_table)


def silu_slope(pre_act):
    sigmoid = jax.nn.sigmoid(pre_act)
    return sigmoid * (1.0 + pre_act * (1.0 - sigmoid))

def slots_of(flat_ids, owners):
    expert_hot = (flat_ids[:, None] == jnp.arange(owners, dtype=jnp.int32)[None, :]).astype(jnp.int32)
    running = jnp.cumsum(expert_hot, axis=0) - 1
    return lax.optimization_barrier(jnp.sum(running * expert_hot, axis=1)).astype(jnp.int32)

def expert_hidden(inputs, up_local):
    pre_act = jnp.dot(inputs, up_local, preferred_element_type=jnp.float32)
    return (pre_act, jax.nn.silu(pre_act).astype(jnp.bfloat16))

def reference(tokens, route_ids, route_weights, up_weight, down_weight, head_weight, out_weight, pool_ids, list_ids, clicks, ranks, alpha_table, beta_table):
    owners = N_EXPERT
    slot_total = owners * CAP
    assign_row = owners * TOK_DEV * TOP
    rows_all = N_DP * owners
    tok_all = tokens.reshape(N_DP, owners * TOK_DEV, D)
    ids_all = route_ids.reshape(N_DP, owners, TOK_DEV * TOP)
    weights_all = route_weights.reshape(N_DP, owners * TOK_DEV, TOP)
    slot_all = jax.vmap(jax.vmap(lambda flat: slots_of(flat, owners)))(ids_all)
    source = jnp.arange(owners, dtype=jnp.int32)[None, :, None]
    place = (ids_all * slot_total + source * CAP + slot_all).reshape(N_DP, assign_row).astype(jnp.int32)
    token_of = jnp.arange(assign_row, dtype=jnp.int32) // TOP

    def buffer_of(row_index):
        rows_in = tok_all[row_index]
        filled = jnp.zeros((owners * slot_total, D), jnp.bfloat16).at[place[row_index]].set(rows_in[token_of])
        return filled.reshape(owners, slot_total, D)

    def one_output(packed):
        inputs, up_local, down_local = packed
        pre_act, activated = expert_hidden(inputs, up_local)
        return lax.dot_general(activated, down_local, (((1,), (1,)), ((), ())), preferred_element_type=jnp.float32).astype(jnp.bfloat16)

    def routed_row(row_index):
        outputs = lax.map(one_output, (buffer_of(row_index), up_weight, down_weight))
        picked = outputs.reshape(owners * slot_total, D)[place[row_index]].reshape(owners * TOK_DEV, TOP, D)
        return lax.optimization_barrier(jnp.sum(weights_all[row_index][:, :, None] * picked.astype(jnp.float32), axis=1))
    routed = lax.map(routed_row, jnp.arange(N_DP, dtype=jnp.int32))
    mixed = (tok_all.astype(jnp.float32) + routed).reshape(rows_all, TOK_DEV, D)
    inv_rms = lax.rsqrt(lax.optimization_barrier(jnp.mean(mixed * mixed, axis=2, keepdims=True)) + 1e-06)
    normed = mixed * inv_rms
    member = (pool_ids[..., None] == jnp.arange(CAND_DEV, dtype=jnp.int32)).astype(jnp.float32)
    token_counts = lax.optimization_barrier(jnp.sum(member, axis=1))
    pooled = (jnp.einsum('ntc,ntd->ncd', member, normed, precision=lax.Precision.HIGHEST) / token_counts[..., None]).astype(jnp.bfloat16)
    pooled_flat = pooled.reshape(rows_all * CAND_DEV, D)
    head_act = jnp.tanh(lax.dot_general(pooled_flat, head_weight, (((1,), (1,)), ((), ())), preferred_element_type=jnp.float32))
    scores = lax.optimization_barrier(jnp.sum(head_act * out_weight[None, :], axis=1)).reshape(N_DP, owners, CAND_DEV)
    rank_hot = (ranks.reshape(N_DP, owners, CAND_DEV)[..., None] == jnp.arange(RANKS, dtype=jnp.int32)).astype(jnp.float32)
    alpha_of = lax.optimization_barrier(jnp.sum(rank_hot * alpha_table, axis=3))
    beta_of = lax.optimization_barrier(jnp.sum(rank_hot * beta_table, axis=3))
    corrected = (clicks.reshape(N_DP, owners, CAND_DEV).astype(jnp.float32) - beta_of) / alpha_of
    list_hot = (list_ids.reshape(N_DP, owners, CAND_DEV)[..., None] == jnp.arange(LISTS, dtype=jnp.int32)).astype(jnp.float32)
    exp_scores = jnp.exp(scores)
    exp_total = lax.optimization_barrier(jnp.sum(exp_scores[..., None] * list_hot, axis=(0, 2)))
    click_total = lax.optimization_barrier(jnp.sum(corrected[..., None] * list_hot, axis=(0, 2)))
    cross_total = lax.optimization_barrier(jnp.sum((corrected * scores)[..., None] * list_hot, axis=(0, 2)))
    list_loss = lax.optimization_barrier(jnp.sum(click_total * jnp.log(exp_total) - cross_total, axis=1))
    cand_grad = lax.optimization_barrier(jnp.sum(list_hot * (click_total / exp_total)[None, :, None, :], axis=3)) * exp_scores - corrected
    grad_flat = cand_grad.reshape(rows_all * CAND_DEV)
    hid_grad = (grad_flat[:, None] * out_weight[None, :] * (1.0 - head_act * head_act)).astype(jnp.bfloat16)
    grad_head = lax.dot_general(hid_grad, pooled_flat, (((0,), (0,)), ((), ())), preferred_element_type=jnp.float32)
    grad_out = lax.optimization_barrier(jnp.sum(grad_flat[:, None] * head_act, axis=0))
    pooled_grad = jnp.dot(hid_grad, head_weight, preferred_element_type=jnp.float32).reshape(rows_all, CAND_DEV, D)
    normed_grad = jnp.einsum('ntc,ncd->ntd', member, pooled_grad / token_counts[..., None], precision=lax.Precision.HIGHEST)
    mixed_grad = inv_rms * (normed_grad - normed * lax.optimization_barrier(jnp.mean(normed_grad * normed, axis=2, keepdims=True)))
    mixed_grad = mixed_grad.reshape(N_DP, owners * TOK_DEV, D)

    def backward_row(carry, row_index):
        up_sum, down_sum = carry
        buffers = buffer_of(row_index)
        cotangent = (weights_all[row_index][:, :, None] * mixed_grad[row_index][:, None, :]).astype(jnp.bfloat16).reshape(assign_row, D)
        slot_grads = jnp.zeros((owners * slot_total, D), jnp.bfloat16).at[place[row_index]].set(cotangent).reshape(owners, slot_total, D)

        def one_expert(packed):
            inputs, slot_grad, up_local, down_local = packed
            pre_act, activated = expert_hidden(inputs, up_local)
            act_grad = jnp.dot(slot_grad, down_local, preferred_element_type=jnp.float32)
            pre_grad = (act_grad * silu_slope(pre_act)).astype(jnp.bfloat16)
            up_term = lax.dot_general(inputs, pre_grad, (((0,), (0,)), ((), ())), preferred_element_type=jnp.float32).astype(jnp.bfloat16)
            down_term = lax.dot_general(slot_grad, activated, (((0,), (0,)), ((), ())), preferred_element_type=jnp.float32).astype(jnp.bfloat16)
            return (up_term, down_term)
        up_terms, down_terms = lax.map(one_expert, (buffers, slot_grads, up_weight, down_weight))
        return ((up_sum + up_terms.astype(jnp.float32), down_sum + down_terms.astype(jnp.float32)), None)
    start_carry = (jnp.zeros((owners, D, FF), jnp.float32), jnp.zeros((owners, D, FF), jnp.float32))
    (up_sum, down_sum), unused = lax.scan(backward_row, start_carry, jnp.arange(N_DP, dtype=jnp.int32))
    return (up_sum.astype(jnp.bfloat16), down_sum.astype(jnp.bfloat16), grad_head, grad_out, list_loss)
```

```python
import functools

import jax
import jax.numpy as jnp
from jax import lax
from jax.experimental import pallas as pl
from jax.experimental.pallas import tpu as pltpu
from jax.sharding import PartitionSpec as P

LISTS = 8
RANKS = 32
MAIN = 16
OVER = 8
F32 = jnp.float32
BF16 = jnp.bfloat16
MESH = pl.DeviceIdType.MESH


def dot(a, b, ca=1, cb=0):
    return lax.dot_general(a, b, (((ca,), (cb,)), ((), ())), preferred_element_type=F32)


def iota(shape, dim):
    return lax.broadcasted_iota(jnp.int32, shape, dim)


def column(row, size):
    diagonal = iota((size, size), 0) == iota((size, size), 1)
    return jnp.sum(jnp.where(diagonal, jnp.broadcast_to(row, (size, size)), 0.0), axis=1, keepdims=True)


def split(value):
    high = value.astype(BF16)
    return high, (value - high.astype(F32)).astype(BF16)


def kernel(
    n_dp,
    n_exp,
    tok,
    ids,
    wts,
    up,
    down,
    head,
    out_w,
    pool,
    lists,
    clicks,
    ranks,
    alpha,
    beta,
    grad_up,
    grad_down,
    grad_head,
    grad_out,
    loss,
    snd1,
    rcv1,
    snd2,
    rcv2,
    snd3,
    rcv3,
    hot_main,
    hot_over,
    mix_main,
    mix_over,
    mix_main_t,
    mix_over_t,
    x_all,
    g_all,
    pre,
    act,
    pre_grad,
    up_all,
    down_all,
    head_all,
    ow_all,
    up_sum,
    down_sum,
    ring_buf,
    totals,
    hid_snd,
    hid_rcv,
    pooled_all,
    out_snd,
    out_rcv,
    head_term,
    piece_snd,
    piece_rcv,
    whole_piece,
    out_piece,
    a2a_send,
    a2a_recv,
    ring_send,
    ring_recv,
    dp_send,
    dp_recv,
    exp_send,
    exp_recv,
):
    toks, width = tok.shape
    top = ids.shape[1]
    half = width // 2
    cands = lists.shape[1]
    units = head.shape[0]
    hidden = units * n_dp
    group = min(16, n_exp)
    groups = n_exp // group
    g_main, g_over = group * MAIN, group * OVER
    g_rows = g_main + g_over
    me_d = lax.axis_index("dp")
    me_e = lax.axis_index("expert")
    right = lax.rem(me_d + 1, n_dp)
    left = lax.rem(me_d + n_dp - 1, n_dp)

    def over_peers(axis, size, me, do):
        def body(k, carry):
            do(lax.rem(me + k, size))
            return carry

        lax.fori_loop(1, size, body, 0)

    def expert_peers(do):
        over_peers("expert", n_exp, me_e, do)

    def dp_peers(do):
        over_peers("dp", n_dp, me_d, do)

    def remote(src, dst, send, recv, axis, peer):
        return pltpu.make_async_remote_copy(
            src_ref=src,
            dst_ref=dst,
            send_sem=send,
            recv_sem=recv,
            device_id={axis: peer},
            device_id_type=MESH,
        )

    def exchange(n, src, dst, p):
        return remote(src.at[p], dst.at[me_e], a2a_send.at[n, p], a2a_recv.at[n, me_e], "expert", p)

    def arrived(n, src, dst, p):
        remote(src.at[p], dst.at[p], a2a_send.at[n, p], a2a_recv.at[n, p], "expert", p).wait_recv()

    def send_group(n, src, dst, g):
        def body(k, carry):
            p = g * group + lax.rem(me_e + k, group)

            @pl.when(p != me_e)
            def _():
                exchange(n, src, dst, p).start()

            return carry

        lax.fori_loop(0, group, body, 0)

    def keep_own(src, dst):
        dst[pl.ds(me_e, 1)] = src[pl.ds(me_e, 1)]

    def pack(dst, g, main, over):
        peers = pl.ds(g * group, group)
        dst[peers, :, 0:width] = main.astype(BF16).reshape(group, MAIN, width)
        low = over[:, 0:half].reshape(group, OVER, half)
        high = over[:, half:width].reshape(group, OVER, half)
        dst[peers, :, width : width + half] = jnp.concatenate([low, high], axis=1).astype(BF16)

    def unpack(src, g):
        peers = pl.ds(g * group, group)
        main = src[peers, :, 0:width].reshape(g_main, width)
        both = src[peers, :, width : width + half].astype(F32)
        low = both[:, 0:OVER, :].reshape(g_over, half)
        high = both[:, OVER : 2 * OVER, :].reshape(g_over, half)
        return main, jnp.concatenate([low, high], axis=1).astype(BF16)

    with jax.named_scope("greet"):
        barrier = pltpu.get_barrier_semaphore()
        expert_peers(
            lambda p: pl.semaphore_signal(barrier, inc=1, device_id={"expert": p}, device_id_type=MESH)
        )
        dp_peers(lambda p: pl.semaphore_signal(barrier, inc=1, device_id={"dp": p}, device_id_type=MESH))

    with jax.named_scope("slots"):
        up_all[pl.ds(me_d, 1)] = up[...]
        down_all[pl.ds(me_d, 1)] = down[...]
        head_all[pl.ds(me_d, 1)] = head[...].reshape(1, units, width)
        lane = iota((toks, 128), 1)
        named = jnp.zeros((toks, 128), F32)
        weight = jnp.zeros((toks, 128), F32)
        for k in range(top):
            hit = ids[:, k : k + 1] == lane
            named = jnp.where(hit, 1.0, named)
            weight = jnp.where(hit, wts[:, k : k + 1], weight)
        named_t = jnp.transpose(named)[0:n_exp]
        weight_t = jnp.transpose(weight)[0:n_exp]
        earlier = jnp.where(iota((toks, toks), 0) < iota((toks, toks), 1), 1.0, 0.0).astype(BF16)
        slot_t = jnp.where(named_t > 0.5, dot(named_t.astype(BF16), earlier), -1.0)

        def one_hot(first, rows):
            slot = (iota((n_exp, rows, toks), 1) + first).astype(F32)
            return jnp.where(slot_t[:, None, :] == slot, 1.0, 0.0).reshape(n_exp * rows, toks)

        hot_main[...] = one_hot(0, MAIN).astype(BF16)
        hot_over[...] = one_hot(MAIN, OVER).astype(BF16)

        def dispatch(g, carry):
            pack(
                snd1,
                g,
                dot(hot_main[pl.ds(g * g_main, g_main), :], tok[...]),
                dot(hot_over[pl.ds(g * g_over, g_over), :], tok[...]),
            )
            return carry

        lax.fori_loop(0, groups, dispatch, 0)
        parity = lax.rem(me_d, 2)
        own_half = iota((8, 128), 1) // units == parity
        ow_all[pl.ds(me_d, 1)] = jnp.where(own_half, jnp.broadcast_to(out_w[...], (8, 128)), 0.0).reshape(1, 8, 128)
        keep_own(snd1, rcv1)

    with jax.named_scope("barrier_wait"):
        pl.semaphore_wait(barrier, n_exp - 1 + n_dp - 1)

    far = n_dp // 2
    near = n_dp - 1 - far

    def hop(chain, step):
        buf, rows, to_right, steps, sem = chain
        owner = lax.rem(me_d + (n_dp - step if to_right else step), n_dp)
        place = buf.at[owner, rows]
        return remote(
            place, place, ring_send.at[sem, step], ring_recv.at[sem, step], "dp", right if to_right else left
        )

    def came(chain, step):
        buf, rows, to_right, steps, sem = chain
        owner = lax.rem(me_d + (n_dp - 1 - step if to_right else step + 1), n_dp)
        place = buf.at[owner, rows]
        remote(
            place, place, ring_send.at[sem, step], ring_recv.at[sem, step], "dp", right if to_right else left
        ).wait_recv()

    def ring_start(chains):
        for chain in chains:
            hop(chain, 0).start()

    def ring_rest(chains):
        def body(step, carry):
            for chain in chains:
                steps = chain[3]

                @pl.when(step < steps)
                def _(chain=chain, steps=steps):
                    came(chain, step)

                    @pl.when(step + 1 < steps)
                    def _():
                        hop(chain, step + 1).start()

            return carry

        lax.fori_loop(0, far, body, 0)

    def ring_drain(chains):
        for chain in chains:

            def body(step, carry, chain=chain):
                hop(chain, step).wait_send()
                return carry

            lax.fori_loop(0, chain[3], body, 0)

    all_rows = pl.ds(0, units)
    first_rows = pl.ds(0, units // 2)
    last_rows = pl.ds(units // 2, units // 2)
    weight_chains = [
        (up_all, all_rows, True, far, 0),
        (up_all, all_rows, False, near, 1),
        (down_all, all_rows, True, near, 2),
        (down_all, all_rows, False, far, 3),
    ]
    head_chains = [
        (head_all, first_rows, True, far, 4),
        (head_all, first_rows, False, near, 5),
        (head_all, last_rows, True, near, 6),
        (head_all, last_rows, False, far, 7),
    ]

    def push(n, src, dst, p):
        return remote(src, dst.at[me_d], dp_send.at[n, p], dp_recv.at[n, me_d], "dp", p)

    def pushed(n, src, dst, p):
        remote(src, dst.at[p], dp_send.at[n, p], dp_recv.at[n, p], "dp", p).wait_recv()

    with jax.named_scope("dispatch_send"):
        ring_start(weight_chains)
        for g in range(groups):
            send_group(0, snd1, rcv1, g)
        dp_peers(lambda p: push(0, ow_all.at[me_d], ow_all, p).start())

    with jax.named_scope("mix_tables"):
        weight_high, weight_low = split(weight_t)

        def spread(part, hot, rows):
            wide = jnp.broadcast_to(part.astype(F32)[:, None, :], (n_exp, rows, toks))
            return hot[...].astype(F32) * wide.reshape(n_exp * rows, toks)

        def both(hot, rows):
            return jnp.concatenate(
                [spread(weight_high, hot, rows), spread(weight_low, hot, rows)], axis=1
            )

        table = both(hot_main, MAIN)
        mix_main[...] = table.astype(BF16)
        mix_main_t[...] = jnp.transpose(table).astype(BF16)
        table = both(hot_over, OVER)
        mix_over[...] = table.astype(BF16)
        mix_over_t[...] = jnp.transpose(table).astype(BF16)

    with jax.named_scope("weight_ring"):
        ring_rest(weight_chains)

    with jax.named_scope("dispatch_wait"):
        expert_peers(lambda p: arrived(0, snd1, rcv1, p))

    with jax.named_scope("expert_forward"):
        ring_start(head_chains)

        def forward(g, carry):
            main, over = unpack(rcv1, g)
            rows = pl.ds(pl.multiple_of(g * g_rows, 16), g_rows)
            x = jnp.concatenate([main, over], axis=0)
            x_all[rows, :] = x
            up_full = up_all[...].reshape(width, up.shape[2])
            pre_act = dot(x, up_full)
            pre[rows, :] = pre_act
            activated = (pre_act * jax.nn.sigmoid(pre_act)).astype(BF16)
            act[rows, :] = activated
            out = dot(activated, down_all[...].reshape(width, down.shape[2]), 1, 1)
            pack(snd2, g, out[0:g_main], out[g_main:g_rows])
            send_group(1, snd2, rcv2, g)
            return carry

        lax.fori_loop(0, groups, forward, 0)
        keep_own(snd2, rcv2)

    with jax.named_scope("head_ring"):
        ring_rest(head_chains)

    with jax.named_scope("slope"):

        def slope(g, carry):
            rows = pl.ds(pl.multiple_of(g * (g_rows // 4), 16), g_rows // 4)
            pre_act = pre[rows, :]
            sigmoid = jax.nn.sigmoid(pre_act)
            pre[rows, :] = sigmoid * (1.0 + pre_act * (1.0 - sigmoid))
            return carry

        lax.fori_loop(0, groups * 4, slope, 0)
        pool_row = pool[...].astype(F32)
        member_t = jnp.where(iota((cands, toks), 0).astype(F32) == pool_row, 1.0, 0.0)
        counts = jnp.sum(member_t, axis=1, keepdims=True)
        pool_column = column(pool_row, toks)
        member = jnp.where(iota((toks, cands), 1).astype(F32) == pool_column, 1.0, 0.0).astype(BF16)
        member_t = member_t.astype(BF16)
        list_hot = jnp.where(
            iota((cands, 128), 1).astype(F32) == column(lists[...].astype(F32), cands), 1.0, 0.0
        )
        rank_hot = jnp.where(
            iota((cands, RANKS), 1).astype(F32) == column(ranks[...].astype(F32), cands), 1.0, 0.0
        )
        alpha_of = jnp.sum(rank_hot * alpha[...], axis=1, keepdims=True)
        beta_of = jnp.sum(rank_hot * beta[...], axis=1, keepdims=True)
        corrected = (column(clicks[...].astype(F32), cands) - beta_of) / alpha_of
        dp_peers(lambda p: pushed(0, ow_all.at[me_d], ow_all, p))
        ow_row = jnp.concatenate(
            [(ow_all[2 * k] + ow_all[2 * k + 1])[0:1] for k in range(hidden // 128)], axis=1
        )

    with jax.named_scope("return_wait"):
        expert_peers(lambda p: arrived(1, snd2, rcv2, p))

    with jax.named_scope("mix"):
        stacked = jnp.zeros((2 * toks, width), F32)
        for g in range(groups):
            main, over = unpack(rcv2, g)
            stacked = stacked + dot(mix_main_t[:, g * g_main : (g + 1) * g_main], main)
            stacked = stacked + dot(mix_over_t[:, g * g_over : (g + 1) * g_over], over)
        mixed = tok[...].astype(F32) + (stacked[0:toks] + stacked[toks : 2 * toks])
        inv_rms = lax.rsqrt(jnp.mean(mixed * mixed, axis=1, keepdims=True) + 1e-06)
        normed = mixed * inv_rms
        normed_high, normed_low = split(normed)
        pooled_sum = dot(member_t, normed_high) + dot(member_t, normed_low)
        pooled = (pooled_sum / counts).astype(BF16)
    with jax.named_scope("head_forward"):
        head_act = jnp.tanh(dot(pooled, head_all[...].reshape(hidden, width), 1, 1))
        scores = jnp.sum(head_act * ow_row, axis=1, keepdims=True)
        exp_scores = jnp.exp(scores)
        tile_row = iota((8, 128), 0)
        terms = jnp.zeros((8, 128), F32)
        for k, value in enumerate((exp_scores, corrected, corrected * scores)):
            terms = jnp.where(tile_row == k, jnp.sum(value * list_hot, axis=0, keepdims=True), terms)
        totals[pl.ds(me_d, 1)] = terms.reshape(1, 8, 128)
    with jax.named_scope("totals"):
        dp_peers(lambda p: push(1, totals.at[me_d], totals, p).start())
        dp_peers(lambda p: pushed(1, totals.at[me_d], totals, p))
    with jax.named_scope("head_backward"):
        total = jnp.sum(totals[...], axis=0)
        in_list = iota((1, 128), 1) < LISTS
        exp_total = jnp.where(in_list, total[0:1], 1.0)
        click_total = jnp.where(in_list, total[1:2], 0.0)
        cross_total = jnp.where(in_list, total[2:3], 0.0)
        loss[...] = jnp.sum(click_total * jnp.log(exp_total) - cross_total, axis=1, keepdims=True)
        ratio = jnp.sum(list_hot * (click_total / exp_total), axis=1, keepdims=True)
        cand_grad = ratio * exp_scores - corrected
        hid_grad = (cand_grad * ow_row * (1.0 - head_act * head_act)).astype(BF16)
        pooled_grad = dot(hid_grad, head_all[...].reshape(hidden, width)) / counts
        grad_high, grad_low = split(pooled_grad)
        normed_grad = dot(member, grad_high) + dot(member, grad_low)
        mixed_grad = inv_rms * (normed_grad - normed * jnp.mean(normed_grad * normed, axis=1, keepdims=True))
        once = mixed_grad.astype(BF16)
        twice = jnp.concatenate([once, once], axis=0)
    with jax.named_scope("grad_send"):
        for g in range(groups):
            pack(
                snd3,
                g,
                dot(mix_main[g * g_main : (g + 1) * g_main, :], twice),
                dot(mix_over[g * g_over : (g + 1) * g_over, :], twice),
            )
            send_group(2, snd3, rcv3, g)
        keep_own(snd3, rcv3)

        out_term = jnp.sum(cand_grad * head_act, axis=0, keepdims=True)
        for k in range(hidden // 128):
            hid_snd[k] = hid_grad[:, k * 128 : (k + 1) * 128]
            out_snd[k] = jnp.broadcast_to(out_term[:, k * 128 : (k + 1) * 128], (8, 128))
        pooled_all[pl.ds(me_d, 1)] = pooled.reshape(1, cands, width)
        hid_rcv[pl.ds(me_d, 1)] = hid_snd[pl.ds(me_d // 2, 1)]
        out_rcv[pl.ds(me_d, 1)] = out_snd[pl.ds(me_d // 2, 1)]

        def send_terms(p):
            push(2, hid_snd.at[p // 2], hid_rcv, p).start()
            push(3, out_snd.at[p // 2], out_rcv, p).start()
            push(4, pooled_all.at[me_d], pooled_all, p).start()

        dp_peers(send_terms)

    with jax.named_scope("grad_wait"):
        expert_peers(lambda p: arrived(2, snd3, rcv3, p))

    tile = min(256, width)
    blocks = tile // units

    def term(dst, a, b):
        def body(f, carry):
            part = dot(a[:, pl.ds(pl.multiple_of(f * tile, 128), tile)], b[...], 0, 0)
            dst[pl.ds(f * blocks, blocks)] = part.astype(BF16).reshape(blocks, units, b.shape[1])
            return carry

        lax.fori_loop(0, width // tile, body, 0)

    def sum_hop(chain, step):
        own, to_right, steps, sem, slot = chain
        if isinstance(step, int) and step == 0:
            owner = lax.rem(me_d + (steps if to_right else n_dp - steps), n_dp)
            src = own.at[owner]
        else:
            src = ring_buf.at[slot, step - 1]
        return remote(
            src,
            ring_buf.at[slot, step],
            ring_send.at[sem, step],
            ring_recv.at[sem, step],
            "dp",
            right if to_right else left,
        )

    def sum_came(chain, step):
        own, to_right, steps, sem, slot = chain
        place = ring_buf.at[slot, step]
        remote(
            place, place, ring_send.at[sem, step], ring_recv.at[sem, step], "dp", right if to_right else left
        ).wait_recv()

    up_chains = [(up_sum, True, far, 8, 0), (up_sum, False, near, 9, 1)]
    down_chains = [(down_sum, True, near, 10, 2), (down_sum, False, far, 11, 3)]

    with jax.named_scope("down_term"):

        def gather(g, carry):
            main, over = unpack(rcv3, g)
            rows = pl.ds(pl.multiple_of(g * g_rows, 16), g_rows)
            g_all[rows, :] = jnp.concatenate([main, over], axis=0)
            return carry

        lax.fori_loop(0, groups, gather, 0)
        term(down_sum, g_all, act)
        for chain in down_chains:
            sum_hop(chain, 0).start()

    with jax.named_scope("up_term"):

        def backward(g, carry):
            rows = pl.ds(pl.multiple_of(g * g_rows, 16), g_rows)
            act_grad = dot(g_all[rows, :], down_all[...].reshape(width, down.shape[2]))
            pre_grad[rows, :] = (act_grad * pre[rows, :]).astype(BF16)
            return carry

        lax.fori_loop(0, groups, backward, 0)
        term(up_sum, x_all, pre_grad)
        for chain in up_chains:
            sum_hop(chain, 0).start()

    columns = width // 128
    with jax.named_scope("head_term"):

        def got_terms(p):
            pushed(2, hid_snd.at[p // 2], hid_rcv, p)
            pushed(3, out_snd.at[p // 2], out_rcv, p)
            pushed(4, pooled_all.at[me_d], pooled_all, p)

        dp_peers(got_terms)
        head_term[...] = dot(
            hid_rcv[...].reshape(n_dp * cands, 128), pooled_all[...].reshape(n_dp * cands, width), 0, 0
        )
        mine = head_term[pl.ds(pl.multiple_of(parity * units, 8), units), :].astype(BF16)
        for q in range(n_exp):
            a, b = q // columns, q % columns
            piece_snd[q] = mine[a * 16 : (a + 1) * 16, b * 128 : (b + 1) * 128]
        piece_rcv[pl.ds(me_e, 1)] = piece_snd[pl.ds(me_e, 1)]
        out_piece[pl.ds(me_e, 1)] = jnp.sum(out_rcv[...], axis=0).reshape(1, 8, 128)

    def piece(p):
        return remote(piece_snd.at[p], piece_rcv.at[me_e], exp_send.at[0, p], exp_recv.at[0, me_e], "expert", p)

    def out_push(p):
        return remote(out_piece.at[me_e], out_piece.at[me_e], exp_send.at[1, p], exp_recv.at[1, me_e], "expert", p)

    def whole_push(p):
        return remote(whole_piece.at[me_e], whole_piece.at[me_e], exp_send.at[2, p], exp_recv.at[2, me_e], "expert", p)

    def got(n, ref, p):
        remote(ref.at[p], ref.at[p], exp_send.at[n, p], exp_recv.at[n, p], "expert", p).wait_recv()

    def send_pieces(p):
        piece(p).start()
        out_push(p).start()

    expert_peers(send_pieces)

    def sum_steps(first, last):
        def body(step, carry):
            for chain in down_chains + up_chains:
                own, to_right, steps, sem, slot = chain

                @pl.when(step + 1 < steps)
                def _(chain=chain):
                    own, to_right, steps, sem, slot = chain
                    sum_came(chain, step)
                    owner = lax.rem(
                        me_d + (steps - 1 - step if to_right else n_dp - (steps - 1) + step), n_dp
                    )
                    total = ring_buf[slot, pl.ds(step, 1)].astype(F32) + own[pl.ds(owner, 1)].astype(F32)
                    ring_buf[slot, pl.ds(step, 1)] = total.astype(BF16)
                    sum_hop(chain, step + 1).start()

            return carry

        lax.fori_loop(first, last, body, 0)

    with jax.named_scope("sum_ring_first"):
        middle = min(3, far - 1)
        sum_steps(0, middle)

    with jax.named_scope("head_pieces"):
        expert_peers(lambda p: got(0, piece_rcv, p))
        whole_piece[pl.ds(me_e, 1)] = jnp.sum(piece_rcv[...].astype(F32), axis=0).reshape(1, 16, 128)
        expert_peers(lambda p: whole_push(p).start())

    with jax.named_scope("sum_ring_last"):
        sum_steps(middle, far - 1)

    with jax.named_scope("head_out"):
        expert_peers(lambda p: got(1, out_piece, p))
        out_all = jnp.sum(out_piece[...], axis=0)[0:1]
        out_pair = jnp.where(parity == 0, out_all, pltpu.roll(out_all, 128 - units, 1))
        grad_out[...] = out_pair[:, 0:units]
        expert_peers(lambda p: got(2, whole_piece, p))
        for q in range(n_exp):
            a, b = q // columns, q % columns
            grad_head[a * 16 : (a + 1) * 16, b * 128 : (b + 1) * 128] = whole_piece[q]

    with jax.named_scope("sum_end"):
        for dst, chains in ((grad_down, down_chains), (grad_up, up_chains)):
            total = chains[0][0][pl.ds(me_d, 1)].astype(F32)
            for chain in chains:
                own, to_right, steps, sem, slot = chain
                sum_came(chain, steps - 1)
                total = total + ring_buf[slot, steps - 1].astype(F32)[None]
            dst[...] = total.astype(BF16)

    with jax.named_scope("drain"):

        def drain_expert(p):
            exchange(0, snd1, rcv1, p).wait_send()
            exchange(1, snd2, rcv2, p).wait_send()
            exchange(2, snd3, rcv3, p).wait_send()
            piece(p).wait_send()
            out_push(p).wait_send()
            whole_push(p).wait_send()

        expert_peers(drain_expert)

        def drain_dp(p):
            push(0, ow_all.at[me_d], ow_all, p).wait_send()
            push(1, totals.at[me_d], totals, p).wait_send()
            push(2, hid_snd.at[p // 2], hid_rcv, p).wait_send()
            push(3, out_snd.at[p // 2], out_rcv, p).wait_send()
            push(4, pooled_all.at[me_d], pooled_all, p).wait_send()

        dp_peers(drain_dp)
        ring_drain(weight_chains + head_chains)
        for chain in down_chains + up_chains:
            sum_hop(chain, 0).wait_send()

            def body(step, carry, chain=chain):
                sum_hop(chain, step).wait_send()
                return carry

            lax.fori_loop(1, chain[2], body, 0)


def local(
    tokens,
    route_ids,
    route_weights,
    up_weight,
    down_weight,
    head_weight,
    out_weight,
    pool_ids,
    list_ids,
    clicks,
    ranks,
    alpha_table,
    beta_table,
):
    n_dp = lax.axis_size("dp")
    n_exp = lax.axis_size("expert")
    toks, width = tokens.shape
    ff = up_weight.shape[2]
    units = head_weight.shape[0]
    cands = list_ids.shape[1]
    slots = n_exp * (MAIN + OVER)
    wire = pltpu.VMEM((n_exp, MAIN, width + width // 2), BF16)
    steps = n_dp // 2
    pairs = units * n_dp // 128
    vmem = pl.BlockSpec(memory_space=pltpu.VMEM)
    outs = pl.pallas_call(
        functools.partial(kernel, n_dp, n_exp),
        out_shape=(
            jax.ShapeDtypeStruct(up_weight.shape, BF16),
            jax.ShapeDtypeStruct(down_weight.shape, BF16),
            jax.ShapeDtypeStruct(head_weight.shape, F32),
            jax.ShapeDtypeStruct((1, units), F32),
            jax.ShapeDtypeStruct((1, 1), F32),
        ),
        in_specs=[vmem] * 13,
        out_specs=(vmem,) * 5,
        scratch_shapes=[
            wire,
            wire,
            wire,
            wire,
            wire,
            wire,
            pltpu.VMEM((n_exp * MAIN, toks), BF16),
            pltpu.VMEM((n_exp * OVER, toks), BF16),
            pltpu.VMEM((n_exp * MAIN, 2 * toks), BF16),
            pltpu.VMEM((n_exp * OVER, 2 * toks), BF16),
            pltpu.VMEM((2 * toks, n_exp * MAIN), BF16),
            pltpu.VMEM((2 * toks, n_exp * OVER), BF16),
            pltpu.VMEM((slots, width), BF16),
            pltpu.VMEM((slots, width), BF16),
            pltpu.VMEM((slots, ff), F32),
            pltpu.VMEM((slots, ff), BF16),
            pltpu.VMEM((slots, ff), BF16),
            pltpu.VMEM((n_dp, width // n_dp, ff), BF16),
            pltpu.VMEM((n_dp, width // n_dp, ff), BF16),
            pltpu.VMEM((n_dp, units, width), BF16),
            pltpu.VMEM((n_dp, 8, 128), F32),
            pltpu.VMEM((n_dp, width // n_dp, ff), BF16),
            pltpu.VMEM((n_dp, width // n_dp, ff), BF16),
            pltpu.VMEM((4, steps, width // n_dp, ff), BF16),
            pltpu.VMEM((n_dp, 8, 128), F32),
            pltpu.VMEM((pairs, cands, 128), BF16),
            pltpu.VMEM((n_dp, cands, 128), BF16),
            pltpu.VMEM((n_dp, cands, width), BF16),
            pltpu.VMEM((pairs, 8, 128), F32),
            pltpu.VMEM((n_dp, 8, 128), F32),
            pltpu.VMEM((128, width), F32),
            pltpu.VMEM((n_exp, 16, 128), BF16),
            pltpu.VMEM((n_exp, 16, 128), BF16),
            pltpu.VMEM((n_exp, 16, 128), F32),
            pltpu.VMEM((n_exp, 8, 128), F32),
            pltpu.SemaphoreType.DMA((3, n_exp)),
            pltpu.SemaphoreType.DMA((3, n_exp)),
            pltpu.SemaphoreType.DMA((12, steps)),
            pltpu.SemaphoreType.DMA((12, steps)),
            pltpu.SemaphoreType.DMA((5, n_dp)),
            pltpu.SemaphoreType.DMA((5, n_dp)),
            pltpu.SemaphoreType.DMA((3, n_exp)),
            pltpu.SemaphoreType.DMA((3, n_exp)),
        ],
        compiler_params=pltpu.CompilerParams(
            collective_id=0, has_side_effects=True, vmem_limit_bytes=56 * 1024 * 1024
        ),
    )(
        tokens,
        route_ids,
        route_weights,
        up_weight,
        down_weight,
        head_weight,
        jnp.concatenate([out_weight, out_weight]).reshape(1, 2 * units),
        pool_ids,
        list_ids,
        clicks,
        ranks,
        alpha_table.reshape(1, RANKS),
        beta_table.reshape(1, RANKS),
    )
    grad_up, grad_down, grad_head, grad_out, list_loss = outs
    return grad_up, grad_down, grad_head, grad_out.reshape(units), list_loss.reshape(1)


def solution(mesh):
    return jax.shard_map(
        local,
        mesh=mesh,
        in_specs=(
            P(("dp", "expert"), None),
            P(("dp", "expert"), None),
            P(("dp", "expert"), None),
            P("expert", "dp", None),
            P("expert", "dp", None),
            P("dp", None),
            P("dp"),
            P(("dp", "expert"), None),
            P(("dp", "expert"), None),
            P(("dp", "expert"), None),
            P(("dp", "expert"), None),
            P(),
            P(),
        ),
        out_specs=(
            P("expert", "dp", None),
            P("expert", "dp", None),
            P("dp", None),
            P("dp"),
            P("expert"),
        ),
        check_vma=False,
    )
```

```python
import functools

import jax
import jax.numpy as jnp
from jax import lax
from jax.experimental import pallas as pl
from jax.experimental.pallas import tpu as pltpu
from jax.sharding import PartitionSpec as P

LISTS = 8
RANKS = 32
MAIN = 16
OVER = 8
F32 = jnp.float32
BF16 = jnp.bfloat16
MESH = pl.DeviceIdType.MESH


def dot(a, b, ca=1, cb=0):
    return lax.dot_general(a, b, (((ca,), (cb,)), ((), ())), preferred_element_type=F32)


def iota(shape, dim):
    return lax.broadcasted_iota(jnp.int32, shape, dim)


def column(row, size):
    diagonal = iota((size, size), 0) == iota((size, size), 1)
    return jnp.sum(jnp.where(diagonal, jnp.broadcast_to(row, (size, size)), 0.0), axis=1, keepdims=True)


def split(value):
    high = value.astype(BF16)
    return high, (value - high.astype(F32)).astype(BF16)


def kernel(
    n_dp,
    n_exp,
    tok,
    ids,
    wts,
    up,
    down,
    head,
    out_w,
    pool,
    lists,
    clicks,
    ranks,
    alpha,
    beta,
    grad_up,
    grad_down,
    grad_head,
    grad_out,
    loss,
    snd1,
    rcv1,
    snd2,
    rcv2,
    snd3,
    rcv3,
    hot_main,
    hot_over,
    mix_main,
    mix_over,
    mix_main_t,
    mix_over_t,
    x_all,
    g_all,
    pre,
    act,
    pre_grad,
    wide_all,
    rest_all,
    down_full,
    head_all,
    ow_all,
    up_sum,
    down_sum,
    up_ring,
    down_ring,
    totals,
    hid_snd,
    hid_rcv,
    pooled_all,
    out_snd,
    out_rcv,
    head_term,
    piece_snd,
    piece_rcv,
    whole_piece,
    out_piece,
    a2a_send,
    a2a_recv,
    ring_send,
    ring_recv,
    dp_send,
    dp_recv,
    exp_send,
    exp_recv,
    twin_send,
    twin_recv,
):
    toks, width = tok.shape
    top = ids.shape[0]
    ff = up.shape[2]
    lanes = wide_all.shape[2]
    spare = lanes - ff
    rest = rest_all.shape[2]
    half = width // 2
    cands = lists.shape[1]
    units = head.shape[0]
    hidden = units * n_dp
    group = min(16, n_exp)
    groups = n_exp // group
    g_main, g_over = group * MAIN, group * OVER
    g_rows = g_main + g_over
    me_d = lax.axis_index("dp")
    me_e = lax.axis_index("expert")
    right = lax.rem(me_d + 1, n_dp)
    left = lax.rem(me_d + n_dp - 1, n_dp)

    def over_peers(axis, size, me, do):
        def body(k, carry):
            do(lax.rem(me + k, size))
            return carry

        lax.fori_loop(1, size, body, 0)

    def expert_peers(do):
        over_peers("expert", n_exp, me_e, do)

    def dp_peers(do):
        over_peers("dp", n_dp, me_d, do)

    def remote(src, dst, send, recv, axis, peer):
        return pltpu.make_async_remote_copy(
            src_ref=src,
            dst_ref=dst,
            send_sem=send,
            recv_sem=recv,
            device_id={axis: peer},
            device_id_type=MESH,
        )

    def exchange(n, src, dst, p):
        return remote(src.at[p], dst.at[me_e], a2a_send.at[n, p], a2a_recv.at[n, me_e], "expert", p)

    def arrived(n, src, dst, p):
        remote(src.at[p], dst.at[p], a2a_send.at[n, p], a2a_recv.at[n, p], "expert", p).wait_recv()

    def send_group(n, src, dst, g):
        def body(k, carry):
            p = g * group + lax.rem(me_e + k, group)

            @pl.when(p != me_e)
            def _():
                exchange(n, src, dst, p).start()

            return carry

        lax.fori_loop(0, group, body, 0)

    def keep_own(src, dst):
        dst[pl.ds(me_e, 1)] = src[pl.ds(me_e, 1)]

    def pack(dst, g, main, over):
        peers = pl.ds(g * group, group)
        dst[peers, :, 0:width] = main.astype(BF16).reshape(group, MAIN, width)
        low = over[:, 0:half].reshape(group, OVER, half)
        high = over[:, half:width].reshape(group, OVER, half)
        dst[peers, :, width : width + half] = jnp.concatenate([low, high], axis=1).astype(BF16)

    def unpack(src, g):
        peers = pl.ds(g * group, group)
        main = src[peers, :, 0:width].reshape(g_main, width)
        both = src[peers, :, width : width + half].astype(F32)
        low = both[:, 0:OVER, :].reshape(g_over, half)
        high = both[:, OVER : 2 * OVER, :].reshape(g_over, half)
        return main, jnp.concatenate([low, high], axis=1).astype(BF16)

    with jax.named_scope("greet"):
        barrier = pltpu.get_barrier_semaphore()
        expert_peers(
            lambda p: pl.semaphore_signal(barrier, inc=1, device_id={"expert": p}, device_id_type=MESH)
        )
        dp_peers(lambda p: pl.semaphore_signal(barrier, inc=1, device_id={"dp": p}, device_id_type=MESH))

    with jax.named_scope("slots"):
        pad = jnp.zeros((up.shape[1], spare), F32)
        turned = pltpu.roll(jnp.concatenate([down[0].astype(F32), pad], axis=1), lanes - spare, 1)
        up_wide = jnp.concatenate([up[0].astype(F32), pad], axis=1)
        own_wide = jnp.where(iota((up.shape[1], lanes), 1) < ff, up_wide, turned)
        wide_all[pl.ds(me_d, 1)] = own_wide.astype(BF16)[None]
        rest_all[pl.ds(me_d, 1)] = turned[:, 0:rest].astype(BF16)[None]
        head_all[pl.ds(me_d, 1)] = head[...].reshape(1, units, width)
        expert = iota((n_exp, toks), 0)
        named_t = jnp.zeros((n_exp, toks), F32)
        weight_t = jnp.zeros((n_exp, toks), F32)
        for k in range(top):
            hit = ids[k : k + 1, :] == expert
            named_t = jnp.where(hit, 1.0, named_t)
            weight_t = jnp.where(hit, wts[k : k + 1, :], weight_t)
        earlier = jnp.where(iota((toks, toks), 0) < iota((toks, toks), 1), 1.0, 0.0).astype(BF16)
        slot_t = jnp.where(named_t > 0.5, dot(named_t.astype(BF16), earlier), -1.0)

        def one_hot(first, rows):
            slot = (iota((n_exp, rows, toks), 1) + first).astype(F32)
            return jnp.where(slot_t[:, None, :] == slot, 1.0, 0.0).reshape(n_exp * rows, toks)

        hot_main[...] = one_hot(0, MAIN).astype(BF16)
        hot_over[...] = one_hot(MAIN, OVER).astype(BF16)

        def dispatch(g, carry):
            pack(
                snd1,
                g,
                dot(hot_main[pl.ds(g * g_main, g_main), :], tok[...]),
                dot(hot_over[pl.ds(g * g_over, g_over), :], tok[...]),
            )
            return carry

        lax.fori_loop(0, groups, dispatch, 0)
        parity = lax.rem(me_d, 2)
        own_row = jnp.concatenate([out_w[...], jnp.zeros((1, 128 - units), F32)], axis=1)
        own_row = jnp.where(parity == 0, own_row, pltpu.roll(own_row, units, 1))
        ow_all[pl.ds(me_d, 1)] = jnp.broadcast_to(own_row, (8, 128))[None]
        keep_own(snd1, rcv1)

    with jax.named_scope("barrier_wait"):
        pl.semaphore_wait(barrier, n_exp - 1 + n_dp - 1)

    far = n_dp // 2
    near = n_dp - 1 - far

    def hop(chain, step):
        buf, rows, to_right, steps, sem = chain
        owner = lax.rem(me_d + (n_dp - step if to_right else step), n_dp)
        place = buf.at[owner, rows]
        return remote(
            place, place, ring_send.at[sem, step], ring_recv.at[sem, step], "dp", right if to_right else left
        )

    def came(chain, step):
        buf, rows, to_right, steps, sem = chain
        owner = lax.rem(me_d + (n_dp - 1 - step if to_right else step + 1), n_dp)
        place = buf.at[owner, rows]
        remote(
            place, place, ring_send.at[sem, step], ring_recv.at[sem, step], "dp", right if to_right else left
        ).wait_recv()

    def ring_start(chains):
        for chain in chains:
            hop(chain, 0).start()

    def ring_step(chains, step, each):
        for chain in chains:
            steps = chain[3]

            @pl.when(step < steps)
            def _(chain=chain, steps=steps):
                came(chain, step)

                @pl.when(step + 1 < steps)
                def _():
                    hop(chain, step + 1).start()

                if each is not None:
                    each(chain, step).start()

    def ring_steps(chains, first, last, each=None):
        def body(step, carry):
            ring_step(chains, step, each)
            return carry

        if first < last:
            lax.fori_loop(first, last, body, 0)

    def ring_drain(chains):
        for chain in chains:

            def body(step, carry, chain=chain):
                hop(chain, step).wait_send()
                return carry

            lax.fori_loop(0, chain[3], body, 0)

    upper = pl.ds(0, units // 2)
    lower = pl.ds(units // 2, units // 2)
    weight_chains = [
        (wide_all, upper, True, far, 0),
        (wide_all, upper, False, near, 1),
        (wide_all, lower, True, near, 2),
        (wide_all, lower, False, far, 3),
        (rest_all, upper, True, far, 4),
        (rest_all, upper, False, near, 5),
        (rest_all, lower, True, near, 6),
        (rest_all, lower, False, far, 7),
    ]
    core = lax.rem(me_e, 2)
    twin = me_e + 1 - 2 * core
    quarter = units // 4

    def head_rows(side, part):
        return pl.ds(pl.multiple_of(side * 2 * quarter + part * quarter, 16), quarter)

    def head_half(side):
        return [
            (head_all, head_rows(side, 0), True, far, 8),
            (head_all, head_rows(side, 0), False, near, 9),
            (head_all, head_rows(side, 1), True, near, 10),
            (head_all, head_rows(side, 1), False, far, 11),
        ]

    head_chains = head_half(core)

    def hand_over(chain, step):
        buf, rows, to_right, steps, sem = chain
        owner = lax.rem(me_d + (n_dp - 1 - step if to_right else step + 1), n_dp)
        place = buf.at[owner, rows]
        return remote(place, place, twin_send.at[sem - 8, step], twin_recv.at[sem - 8, step], "expert", twin)

    def twins(chains, do):
        for chain in chains:

            def body(step, carry, chain=chain):
                do(hand_over(chain, step))
                return carry

            lax.fori_loop(0, chain[3], body, 0)

    pooled_chains = [
        (pooled_all, pl.ds(0, cands), True, far, 20),
        (pooled_all, pl.ds(0, cands), False, near, 21),
    ]

    def push(n, src, dst, p):
        return remote(src, dst.at[me_d], dp_send.at[n, p], dp_recv.at[n, me_d], "dp", p)

    def pushed(n, src, dst, p):
        remote(src, dst.at[p], dp_send.at[n, p], dp_recv.at[n, p], "dp", p).wait_recv()

    with jax.named_scope("dispatch_send"):
        ring_start(weight_chains)
        for g in range(groups):
            send_group(0, snd1, rcv1, g)
        dp_peers(lambda p: push(0, ow_all.at[me_d], ow_all, p).start())

    with jax.named_scope("mix_tables"):
        weight_high, weight_low = split(weight_t)

        def spread(part, hot, rows):
            wide = jnp.broadcast_to(part.astype(F32)[:, None, :], (n_exp, rows, toks))
            return hot[...].astype(F32) * wide.reshape(n_exp * rows, toks)

        def both(hot, rows):
            return jnp.concatenate(
                [spread(weight_high, hot, rows), spread(weight_low, hot, rows)], axis=1
            )

        table = both(hot_main, MAIN)
        mix_main[...] = table.astype(BF16)
        mix_main_t[...] = jnp.transpose(table).astype(BF16)
        table = both(hot_over, OVER)
        mix_over[...] = table.astype(BF16)
        mix_over_t[...] = jnp.transpose(table).astype(BF16)

    with jax.named_scope("weight_ring"):
        ring_steps(weight_chains, 0, far - 1)
        ring_start(head_chains)
        ring_steps(weight_chains, far - 1, far)

    with jax.named_scope("dispatch_wait"):
        expert_peers(lambda p: arrived(0, snd1, rcv1, p))

    with jax.named_scope("expert_forward"):
        ring_step(head_chains, 0, hand_over)
        down_full[:, 0:rest] = rest_all[...].reshape(width, rest)
        down_full[:, rest:lanes] = wide_all[:, :, rest:lanes].reshape(width, lanes - rest)

        def no_column(rows):
            lane = iota((rows, lanes), 1)
            return (lane >= rest) & (lane < rest + spare)

        def forward(g):
            main, over = unpack(rcv1, g)
            rows = pl.ds(g * g_rows, g_rows)
            x = jnp.concatenate([main, over], axis=0)
            x_all[rows, :] = x
            natural = dot(x, wide_all[...].reshape(width, lanes))
            pre_act = jnp.where(no_column(g_rows), 0.0, pltpu.roll(natural, lanes - spare, 1))
            pre[rows, :] = pre_act
            activated = (pre_act * jax.nn.sigmoid(pre_act)).astype(BF16)
            act[rows, :] = activated
            out = dot(activated, down_full[...], 1, 1)
            pack(snd2, g, out[0:g_main], out[g_main:g_rows])
            send_group(1, snd2, rcv2, g)

        head_at = 1
        for g in range(groups):
            forward(g)
            if head_at < far:
                ring_step(head_chains, head_at, hand_over)
                head_at += 1
        keep_own(snd2, rcv2)

    with jax.named_scope("head_ring"):
        ring_steps(head_chains, head_at, far, hand_over)
        twins(head_half(1 - core), lambda copy: copy.wait_recv())

    with jax.named_scope("slope"):

        def slope(g, carry):
            rows = pl.ds(pl.multiple_of(g * (g_rows // 4), 16), g_rows // 4)
            pre_act = pre[rows, :]
            sigmoid = jax.nn.sigmoid(pre_act)
            slope_of = sigmoid * (1.0 + pre_act * (1.0 - sigmoid))
            pre[rows, :] = jnp.where(no_column(g_rows // 4), 0.0, slope_of)
            return carry

        lax.fori_loop(0, groups * 4, slope, 0)
        pool_row = pool[...].astype(F32)
        member_t = jnp.where(iota((cands, toks), 0).astype(F32) == pool_row, 1.0, 0.0)
        counts = jnp.sum(member_t, axis=1, keepdims=True)
        pool_column = column(pool_row, toks)
        member = jnp.where(iota((toks, cands), 1).astype(F32) == pool_column, 1.0, 0.0).astype(BF16)
        member_t = member_t.astype(BF16)
        list_hot = jnp.where(
            iota((cands, 128), 1).astype(F32) == column(lists[...].astype(F32), cands), 1.0, 0.0
        )
        rank_hot = jnp.where(
            iota((cands, RANKS), 1).astype(F32) == column(ranks[...].astype(F32), cands), 1.0, 0.0
        )
        alpha_of = jnp.sum(rank_hot * alpha[...], axis=1, keepdims=True)
        beta_of = jnp.sum(rank_hot * beta[...], axis=1, keepdims=True)
        corrected = (column(clicks[...].astype(F32), cands) - beta_of) / alpha_of
        dp_peers(lambda p: pushed(0, ow_all.at[me_d], ow_all, p))
        ow_row = jnp.concatenate(
            [(ow_all[2 * k] + ow_all[2 * k + 1])[0:1] for k in range(hidden // 128)], axis=1
        )

    with jax.named_scope("return_wait"):
        expert_peers(lambda p: arrived(1, snd2, rcv2, p))

    with jax.named_scope("mix"):
        stacked = jnp.zeros((2 * toks, width), F32)
        for g in range(groups):
            main, over = unpack(rcv2, g)
            stacked = stacked + dot(mix_main_t[:, g * g_main : (g + 1) * g_main], main)
            stacked = stacked + dot(mix_over_t[:, g * g_over : (g + 1) * g_over], over)
        mixed = tok[...].astype(F32) + (stacked[0:toks] + stacked[toks : 2 * toks])
        inv_rms = lax.rsqrt(jnp.mean(mixed * mixed, axis=1, keepdims=True) + 1e-06)
        normed = mixed * inv_rms
        normed_high, normed_low = split(normed)
        pooled_sum = dot(member_t, normed_high) + dot(member_t, normed_low)
        pooled = (pooled_sum / counts).astype(BF16)
        pooled_all[pl.ds(me_d, 1)] = pooled.reshape(1, cands, width)
        ring_start(pooled_chains)
    with jax.named_scope("head_forward"):
        head_act = jnp.tanh(dot(pooled, head_all[...].reshape(hidden, width), 1, 1))
        scores = jnp.sum(head_act * ow_row, axis=1, keepdims=True)
        exp_scores = jnp.exp(scores)
        tile_row = iota((8, 128), 0)
        terms = jnp.zeros((8, 128), F32)
        for k, value in enumerate((exp_scores, corrected, corrected * scores)):
            terms = jnp.where(tile_row == k, jnp.sum(value * list_hot, axis=0, keepdims=True), terms)
        totals[pl.ds(me_d, 1)] = terms.reshape(1, 8, 128)
    with jax.named_scope("totals"):
        dp_peers(lambda p: push(1, totals.at[me_d], totals, p).start())
        pooled_at = min(2, far)
        ring_steps(pooled_chains, 0, pooled_at)
        dp_peers(lambda p: pushed(1, totals.at[me_d], totals, p))
    with jax.named_scope("head_backward"):
        total = jnp.sum(totals[...], axis=0)
        in_list = iota((1, 128), 1) < LISTS
        exp_total = jnp.where(in_list, total[0:1], 1.0)
        click_total = jnp.where(in_list, total[1:2], 0.0)
        cross_total = jnp.where(in_list, total[2:3], 0.0)
        loss[...] = jnp.sum(click_total * jnp.log(exp_total) - cross_total, axis=1, keepdims=True)
        ratio = jnp.sum(list_hot * (click_total / exp_total), axis=1, keepdims=True)
        cand_grad = ratio * exp_scores - corrected
        hid_grad = (cand_grad * ow_row * (1.0 - head_act * head_act)).astype(BF16)
        pooled_grad = dot(hid_grad, head_all[...].reshape(hidden, width)) / counts
        grad_high, grad_low = split(pooled_grad)
        normed_grad = dot(member, grad_high) + dot(member, grad_low)
        mixed_grad = inv_rms * (normed_grad - normed * jnp.mean(normed_grad * normed, axis=1, keepdims=True))
        once = mixed_grad.astype(BF16)
        twice = jnp.concatenate([once, once], axis=0)
    with jax.named_scope("grad_send"):
        for g in range(groups):
            pack(
                snd3,
                g,
                dot(mix_main[g * g_main : (g + 1) * g_main, :], twice),
                dot(mix_over[g * g_over : (g + 1) * g_over, :], twice),
            )
            send_group(2, snd3, rcv3, g)
        keep_own(snd3, rcv3)

        out_term = jnp.sum(cand_grad * head_act, axis=0, keepdims=True)
        for k in range(hidden // 128):
            hid_snd[k] = hid_grad[:, k * 128 : (k + 1) * 128]
            out_snd[k] = jnp.broadcast_to(out_term[:, k * 128 : (k + 1) * 128], (8, 128))
        hid_rcv[pl.ds(me_d, 1)] = hid_snd[pl.ds(me_d // 2, 1)]
        out_rcv[pl.ds(me_d, 1)] = out_snd[pl.ds(me_d // 2, 1)]

        def send_terms(p):
            push(2, hid_snd.at[p // 2], hid_rcv, p).start()
            push(3, out_snd.at[p // 2], out_rcv, p).start()

        dp_peers(send_terms)

    with jax.named_scope("pooled_ring"):
        ring_steps(pooled_chains, pooled_at, far)

    with jax.named_scope("grad_wait"):
        expert_peers(lambda p: arrived(2, snd3, rcv3, p))

    tile = min(256, width)
    blocks = tile // units

    def down_part(f, carry):
        part = dot(g_all[:, pl.ds(pl.multiple_of(f * tile, 128), tile)], act[...], 0, 0)
        place = pl.ds(f * blocks, blocks)
        down_sum[place] = part[:, 0:rest].astype(BF16).reshape(blocks, units, rest)
        up_sum[place, :, rest:lanes] = part[:, rest:lanes].astype(BF16).reshape(blocks, units, lanes - rest)
        return carry

    def up_part(f, carry):
        part = dot(x_all[:, pl.ds(pl.multiple_of(f * tile, 128), tile)], pre_grad[...], 0, 0)
        place = pl.ds(f * blocks, blocks)
        up_sum[place, :, 0:rest] = part[:, 0:rest].astype(BF16).reshape(blocks, units, rest)
        below = up_sum[place, :, rest:lanes].astype(F32).reshape(tile, lanes - rest)
        last = jnp.where(iota(below.shape, 1) < spare, pltpu.roll(below, spare, 1), part[:, rest:lanes])
        up_sum[place, :, rest:lanes] = last.astype(BF16).reshape(blocks, units, lanes - rest)
        return carry

    def sum_hop(chain, step):
        own, ring, to_right, steps, sem, slot, rows = chain
        if isinstance(step, int) and step == 0:
            owner = lax.rem(me_d + (steps if to_right else n_dp - steps), n_dp)
            src = own.at[owner, rows]
        else:
            src = ring.at[slot, step - 1, rows]
        return remote(
            src,
            ring.at[slot, step, rows],
            ring_send.at[sem, step],
            ring_recv.at[sem, step],
            "dp",
            right if to_right else left,
        )

    def sum_came(chain, step):
        own, ring, to_right, steps, sem, slot, rows = chain
        place = ring.at[slot, step, rows]
        remote(
            place, place, ring_send.at[sem, step], ring_recv.at[sem, step], "dp", right if to_right else left
        ).wait_recv()

    def sum_chains(own, ring, sem):
        return [
            (own, ring, True, far, sem, 0, upper),
            (own, ring, False, near, sem + 1, 1, upper),
            (own, ring, True, near, sem + 2, 0, lower),
            (own, ring, False, far, sem + 3, 1, lower),
        ]

    up_chains = sum_chains(up_sum, up_ring, 12)
    down_chains = sum_chains(down_sum, down_ring, 16)

    with jax.named_scope("down_term"):

        def gather(g, carry):
            main, over = unpack(rcv3, g)
            rows = pl.ds(pl.multiple_of(g * g_rows, 16), g_rows)
            g_all[rows, :] = jnp.concatenate([main, over], axis=0)
            return carry

        lax.fori_loop(0, groups, gather, 0)
        lax.fori_loop(0, width // tile, down_part, 0)
        for chain in down_chains:
            sum_hop(chain, 0).start()

    with jax.named_scope("up_term"):

        def backward(g, carry):
            rows = pl.ds(pl.multiple_of(g * g_rows, 16), g_rows)
            act_grad = dot(g_all[rows, :], down_full[...])
            pre_grad[rows, :] = (act_grad * pre[rows, :]).astype(BF16)
            return carry

        lax.fori_loop(0, groups, backward, 0)
        lax.fori_loop(0, width // tile, up_part, 0)
        for chain in up_chains:
            sum_hop(chain, 0).start()

    columns = width // 128
    with jax.named_scope("head_term"):

        def got_terms(p):
            pushed(2, hid_snd.at[p // 2], hid_rcv, p)
            pushed(3, out_snd.at[p // 2], out_rcv, p)

        dp_peers(got_terms)
        head_term[...] = dot(
            hid_rcv[...].reshape(n_dp * cands, 128), pooled_all[...].reshape(n_dp * cands, width), 0, 0
        )
        mine = head_term[pl.ds(pl.multiple_of(parity * units, 8), units), :].astype(BF16)
        for q in range(n_exp):
            a, b = q // columns, q % columns
            piece_snd[q] = mine[a * 16 : (a + 1) * 16, b * 128 : (b + 1) * 128]
        piece_rcv[pl.ds(me_e, 1)] = piece_snd[pl.ds(me_e, 1)]
        out_piece[pl.ds(me_e, 1)] = jnp.sum(out_rcv[...], axis=0).reshape(1, 8, 128)

    def piece(p):
        return remote(piece_snd.at[p], piece_rcv.at[me_e], exp_send.at[0, p], exp_recv.at[0, me_e], "expert", p)

    def out_push(p):
        return remote(out_piece.at[me_e], out_piece.at[me_e], exp_send.at[1, p], exp_recv.at[1, me_e], "expert", p)

    def whole_push(p):
        return remote(whole_piece.at[me_e], whole_piece.at[me_e], exp_send.at[2, p], exp_recv.at[2, me_e], "expert", p)

    def got(n, ref, p):
        remote(ref.at[p], ref.at[p], exp_send.at[n, p], exp_recv.at[n, p], "expert", p).wait_recv()

    def send_pieces(p):
        piece(p).start()
        out_push(p).start()

    expert_peers(send_pieces)

    def sum_steps(first, last):
        def body(step, carry):
            for chain in down_chains + up_chains:
                steps = chain[3]

                @pl.when(step + 1 < steps)
                def _(chain=chain):
                    own, ring, to_right, steps, sem, slot, rows = chain
                    sum_came(chain, step)
                    owner = lax.rem(
                        me_d + (steps - 1 - step if to_right else n_dp - (steps - 1) + step), n_dp
                    )
                    total = ring[slot, pl.ds(step, 1), rows].astype(F32) + own[pl.ds(owner, 1), rows].astype(F32)
                    ring[slot, pl.ds(step, 1), rows] = total.astype(BF16)
                    sum_hop(chain, step + 1).start()

            return carry

        lax.fori_loop(first, last, body, 0)

    with jax.named_scope("sum_ring_first"):
        middle = min(3, far - 1)
        sum_steps(0, middle)

    with jax.named_scope("head_pieces"):
        expert_peers(lambda p: got(0, piece_rcv, p))
        whole_piece[pl.ds(me_e, 1)] = jnp.sum(piece_rcv[...].astype(F32), axis=0).reshape(1, 16, 128)
        expert_peers(lambda p: whole_push(p).start())

    with jax.named_scope("sum_ring_last"):
        sum_steps(middle, far - 1)

    with jax.named_scope("head_out"):
        expert_peers(lambda p: got(1, out_piece, p))
        out_all = jnp.sum(out_piece[...], axis=0)[0:1]
        out_pair = jnp.where(parity == 0, out_all, pltpu.roll(out_all, 128 - units, 1))
        grad_out[...] = out_pair[:, 0:units]
        expert_peers(lambda p: got(2, whole_piece, p))
        for q in range(n_exp):
            a, b = q // columns, q % columns
            grad_head[a * 16 : (a + 1) * 16, b * 128 : (b + 1) * 128] = whole_piece[q]

    with jax.named_scope("sum_end"):
        sums = []
        for chains in (down_chains, up_chains):
            halves = []
            for pair in (chains[0:2], chains[2:4]):
                total = 0.0
                for chain in pair:
                    own, ring, to_right, steps, sem, slot, rows = chain
                    sum_came(chain, steps - 1)
                    total = total + ring[slot, steps - 1, rows].astype(F32)
                halves.append(total + own[pl.ds(me_d, 1), rows][0].astype(F32))
            sums.append(jnp.concatenate(halves, axis=0))
        most, wide = sums
        grad_up[...] = pltpu.roll(wide, spare, 1)[:, 0:ff].astype(BF16)[None]
        whole = jnp.concatenate([most, pltpu.roll(wide[:, rest:lanes], spare, 1)], axis=1)
        grad_down[...] = pltpu.roll(whole, spare, 1)[:, 0:ff].astype(BF16)[None]

    with jax.named_scope("drain"):

        def drain_expert(p):
            exchange(0, snd1, rcv1, p).wait_send()
            exchange(1, snd2, rcv2, p).wait_send()
            exchange(2, snd3, rcv3, p).wait_send()
            piece(p).wait_send()
            out_push(p).wait_send()
            whole_push(p).wait_send()

        expert_peers(drain_expert)

        def drain_dp(p):
            push(0, ow_all.at[me_d], ow_all, p).wait_send()
            push(1, totals.at[me_d], totals, p).wait_send()
            push(2, hid_snd.at[p // 2], hid_rcv, p).wait_send()
            push(3, out_snd.at[p // 2], out_rcv, p).wait_send()

        dp_peers(drain_dp)
        ring_drain(weight_chains + head_chains + pooled_chains)
        twins(head_chains, lambda copy: copy.wait_send())
        for chain in down_chains + up_chains:
            sum_hop(chain, 0).wait_send()

            def body(step, carry, chain=chain):
                sum_hop(chain, step).wait_send()
                return carry

            lax.fori_loop(1, chain[3], body, 0)


def hand_out(*refs):
    for src, dst in zip(refs[:5], refs[5:]):
        dst[...] = src[...]


def local(
    tokens,
    route_ids,
    route_weights,
    up_weight,
    down_weight,
    head_weight,
    out_weight,
    pool_ids,
    list_ids,
    clicks,
    ranks,
    alpha_table,
    beta_table,
):
    n_dp = lax.axis_size("dp")
    n_exp = lax.axis_size("expert")
    toks, width = tokens.shape
    ff = up_weight.shape[2]
    lanes = -(-ff // 128) * 128
    rest = 2 * ff - lanes
    units = head_weight.shape[0]
    cands = list_ids.shape[1]
    slots = n_exp * (MAIN + OVER)
    wire = pltpu.VMEM((n_exp, MAIN, width + width // 2), BF16)
    steps = n_dp // 2
    pairs = units * n_dp // 128
    vmem = pl.BlockSpec(memory_space=pltpu.VMEM)
    outs = pl.pallas_call(
        functools.partial(kernel, n_dp, n_exp),
        out_shape=(
            jax.ShapeDtypeStruct(up_weight.shape, BF16),
            jax.ShapeDtypeStruct(down_weight.shape, BF16),
            jax.ShapeDtypeStruct(head_weight.shape, F32),
            jax.ShapeDtypeStruct((1, units), F32),
            jax.ShapeDtypeStruct((1, 1), F32),
        ),
        in_specs=[vmem] * 13,
        out_specs=(vmem,) * 5,
        scratch_shapes=[
            wire,
            wire,
            wire,
            wire,
            wire,
            wire,
            pltpu.VMEM((n_exp * MAIN, toks), BF16),
            pltpu.VMEM((n_exp * OVER, toks), BF16),
            pltpu.VMEM((n_exp * MAIN, 2 * toks), BF16),
            pltpu.VMEM((n_exp * OVER, 2 * toks), BF16),
            pltpu.VMEM((2 * toks, n_exp * MAIN), BF16),
            pltpu.VMEM((2 * toks, n_exp * OVER), BF16),
            pltpu.VMEM((slots, width), BF16),
            pltpu.VMEM((slots, width), BF16),
            pltpu.VMEM((slots, lanes), F32),
            pltpu.VMEM((slots, lanes), BF16),
            pltpu.VMEM((slots, lanes), BF16),
            pltpu.VMEM((n_dp, width // n_dp, lanes), BF16),
            pltpu.VMEM((n_dp, width // n_dp, rest), BF16),
            pltpu.VMEM((width, lanes), BF16),
            pltpu.VMEM((n_dp, units, width), BF16),
            pltpu.VMEM((n_dp, 8, 128), F32),
            pltpu.VMEM((n_dp, width // n_dp, lanes), BF16),
            pltpu.VMEM((n_dp, width // n_dp, rest), BF16),
            pltpu.VMEM((2, steps, width // n_dp, lanes), BF16),
            pltpu.VMEM((2, steps, width // n_dp, rest), BF16),
            pltpu.VMEM((n_dp, 8, 128), F32),
            pltpu.VMEM((pairs, cands, 128), BF16),
            pltpu.VMEM((n_dp, cands, 128), BF16),
            pltpu.VMEM((n_dp, cands, width), BF16),
            pltpu.VMEM((pairs, 8, 128), F32),
            pltpu.VMEM((n_dp, 8, 128), F32),
            pltpu.VMEM((128, width), F32),
            pltpu.VMEM((n_exp, 16, 128), BF16),
            pltpu.VMEM((n_exp, 16, 128), BF16),
            pltpu.VMEM((n_exp, 16, 128), F32),
            pltpu.VMEM((n_exp, 8, 128), F32),
            pltpu.SemaphoreType.DMA((3, n_exp)),
            pltpu.SemaphoreType.DMA((3, n_exp)),
            pltpu.SemaphoreType.DMA((22, steps)),
            pltpu.SemaphoreType.DMA((22, steps)),
            pltpu.SemaphoreType.DMA((4, n_dp)),
            pltpu.SemaphoreType.DMA((4, n_dp)),
            pltpu.SemaphoreType.DMA((3, n_exp)),
            pltpu.SemaphoreType.DMA((3, n_exp)),
            pltpu.SemaphoreType.DMA((4, steps)),
            pltpu.SemaphoreType.DMA((4, steps)),
        ],
        compiler_params=pltpu.CompilerParams(
            collective_id=0, has_side_effects=True, vmem_limit_bytes=56 * 1024 * 1024
        ),
    )(
        tokens,
        route_ids.T,
        route_weights.T,
        up_weight,
        down_weight,
        head_weight,
        out_weight.reshape(1, units),
        pool_ids,
        list_ids,
        clicks,
        ranks,
        alpha_table.reshape(1, RANKS),
        beta_table.reshape(1, RANKS),
    )
    grad_up, grad_down, grad_head, grad_out, list_loss = pl.pallas_call(
        hand_out,
        out_shape=[jax.ShapeDtypeStruct(o.shape, o.dtype) for o in outs],
        in_specs=[vmem] * 5,
        out_specs=[vmem] * 5,
    )(*outs)
    return grad_up, grad_down, grad_head, grad_out.reshape(units), list_loss.reshape(1)


def solution(mesh):
    return jax.shard_map(
        local,
        mesh=mesh,
        in_specs=(
            P(("dp", "expert"), None),
            P(("dp", "expert"), None),
            P(("dp", "expert"), None),
            P("expert", "dp", None),
            P("expert", "dp", None),
            P("dp", None),
            P("dp"),
            P(("dp", "expert"), None),
            P(("dp", "expert"), None),
            P(("dp", "expert"), None),
            P(("dp", "expert"), None),
            P(),
            P(),
        ),
        out_specs=(
            P("expert", "dp", None),
            P("expert", "dp", None),
            P("dp", None),
            P("dp"),
            P("expert"),
        ),
        check_vma=False,
    )
```

```python
import functools

import jax
import jax.numpy as jnp
from jax import lax
from jax.experimental import pallas as pl
from jax.experimental.pallas import tpu as pltpu
from jax.sharding import PartitionSpec as P

LISTS = 8
RANKS = 32
MAIN = 16
OVER = 8
F32 = jnp.float32
BF16 = jnp.bfloat16
MESH = pl.DeviceIdType.MESH


def dot(a, b, ca=1, cb=0):
    return lax.dot_general(a, b, (((ca,), (cb,)), ((), ())), preferred_element_type=F32)


def iota(shape, dim):
    return lax.broadcasted_iota(jnp.int32, shape, dim)


def column(row, size):
    diagonal = iota((size, size), 0) == iota((size, size), 1)
    return jnp.sum(jnp.where(diagonal, jnp.broadcast_to(row, (size, size)), 0.0), axis=1, keepdims=True)


def split(value):
    high = value.astype(BF16)
    return high, (value - high.astype(F32)).astype(BF16)


def kernel(
    n_dp,
    n_exp,
    tok,
    ids,
    wts,
    up,
    down,
    head,
    out_w,
    pool,
    lists,
    clicks,
    ranks,
    alpha,
    beta,
    grad_up,
    grad_down,
    grad_head,
    grad_out,
    loss,
    snd1,
    rcv1,
    snd2,
    rcv2,
    snd3,
    rcv3,
    hot_main,
    hot_over,
    mix_main,
    mix_over,
    mix_main_t,
    mix_over_t,
    x_all,
    g_all,
    pre,
    act,
    pre_grad,
    wide_all,
    rest_all,
    down_full,
    head_all,
    ow_all,
    up_sum,
    down_sum,
    up_ring,
    down_ring,
    totals,
    hid_snd,
    hid_rcv,
    pooled_all,
    out_snd,
    out_rcv,
    head_term,
    piece_snd,
    piece_rcv,
    whole_piece,
    out_piece,
    a2a_send,
    a2a_recv,
    ring_send,
    ring_recv,
    dp_send,
    dp_recv,
    exp_send,
    exp_recv,
    twin_send,
    twin_recv,
):
    toks, width = tok.shape
    top = ids.shape[0]
    ff = up.shape[2]
    lanes = wide_all.shape[2]
    spare = lanes - ff
    rest = rest_all.shape[2]
    half = width // 2
    cands = lists.shape[1]
    units = head.shape[0]
    hidden = units * n_dp
    group = min(16, n_exp)
    groups = n_exp // group
    g_main, g_over = group * MAIN, group * OVER
    g_rows = g_main + g_over
    me_d = lax.axis_index("dp")
    me_e = lax.axis_index("expert")
    right = lax.rem(me_d + 1, n_dp)
    left = lax.rem(me_d + n_dp - 1, n_dp)

    def expert_peers(do):
        def body(k, carry):
            do(lax.rem(me_e + k, n_exp))
            return carry

        lax.fori_loop(1, n_exp, body, 0)

    def dp_peers(do):
        def body(k, carry):
            away = n_dp // 2 + ((k + 1) // 2) * (1 - 2 * lax.rem(k, 2))
            do(lax.rem(me_d + away, n_dp))
            return carry

        lax.fori_loop(0, n_dp - 1, body, 0)

    def remote(src, dst, send, recv, axis, peer):
        return pltpu.make_async_remote_copy(
            src_ref=src,
            dst_ref=dst,
            send_sem=send,
            recv_sem=recv,
            device_id={axis: peer},
            device_id_type=MESH,
        )

    def exchange(n, src, dst, p):
        return remote(src.at[p], dst.at[me_e], a2a_send.at[n], a2a_recv.at[n], "expert", p)

    next_e = lax.rem(me_e + 1, n_exp)

    def exchanged(n, src, dst):
        peers = pl.ds(0, n_exp - 1)
        return remote(src.at[peers], dst.at[peers], a2a_send.at[n], a2a_recv.at[n], "expert", next_e)

    def send_group(n, src, dst, g):
        def body(k, carry):
            p = g * group + lax.rem(me_e + k, group)

            @pl.when(p != me_e)
            def _():
                exchange(n, src, dst, p).start()

            return carry

        lax.fori_loop(0, group, body, 0)

    def keep_own(src, dst):
        dst[pl.ds(me_e, 1)] = src[pl.ds(me_e, 1)]

    def pack(dst, g, main, over):
        peers = pl.ds(g * group, group)
        dst[peers, :, 0:width] = main.astype(BF16).reshape(group, MAIN, width)
        low = over[:, 0:half].reshape(group, OVER, half)
        high = over[:, half:width].reshape(group, OVER, half)
        dst[peers, :, width : width + half] = jnp.concatenate([low, high], axis=1).astype(BF16)

    def unpack(src, g):
        peers = pl.ds(g * group, group)
        main = src[peers, :, 0:width].reshape(g_main, width)
        both = src[peers, :, width : width + half].astype(F32)
        low = both[:, 0:OVER, :].reshape(g_over, half)
        high = both[:, OVER : 2 * OVER, :].reshape(g_over, half)
        return main, jnp.concatenate([low, high], axis=1).astype(BF16)

    with jax.named_scope("greet"):
        barrier = pltpu.get_barrier_semaphore()
        expert_peers(
            lambda p: pl.semaphore_signal(barrier, inc=1, device_id={"expert": p}, device_id_type=MESH)
        )
        dp_peers(lambda p: pl.semaphore_signal(barrier, inc=1, device_id={"dp": p}, device_id_type=MESH))

    with jax.named_scope("slots"):
        pad = jnp.zeros((up.shape[1], spare), F32)
        turned = pltpu.roll(jnp.concatenate([down[0].astype(F32), pad], axis=1), lanes - spare, 1)
        up_wide = jnp.concatenate([up[0].astype(F32), pad], axis=1)
        own_wide = jnp.where(iota((up.shape[1], lanes), 1) < ff, up_wide, turned)
        wide_all[pl.ds(me_d, 1)] = own_wide.astype(BF16)[None]
        rest_all[pl.ds(me_d, 1)] = turned[:, 0:rest].astype(BF16)[None]
        head_all[pl.ds(me_d, 1)] = head[...].reshape(1, units, width)
        expert = iota((n_exp, toks), 0)
        named_t = jnp.zeros((n_exp, toks), F32)
        weight_t = jnp.zeros((n_exp, toks), F32)
        for k in range(top):
            hit = ids[k : k + 1, :] == expert
            named_t = jnp.where(hit, 1.0, named_t)
            weight_t = jnp.where(hit, wts[k : k + 1, :], weight_t)
        earlier = jnp.where(iota((toks, toks), 0) < iota((toks, toks), 1), 1.0, 0.0).astype(BF16)
        slot_t = jnp.where(named_t > 0.5, dot(named_t.astype(BF16), earlier), -1.0)

        def one_hot(first, rows):
            slot = (iota((n_exp, rows, toks), 1) + first).astype(F32)
            return jnp.where(slot_t[:, None, :] == slot, 1.0, 0.0).reshape(n_exp * rows, toks)

        hot_main[...] = one_hot(0, MAIN).astype(BF16)
        hot_over[...] = one_hot(MAIN, OVER).astype(BF16)

        def dispatch(g, carry):
            pack(
                snd1,
                g,
                dot(hot_main[pl.ds(g * g_main, g_main), :], tok[...]),
                dot(hot_over[pl.ds(g * g_over, g_over), :], tok[...]),
            )
            return carry

        lax.fori_loop(0, groups, dispatch, 0)
        parity = lax.rem(me_d, 2)
        own_row = jnp.concatenate([out_w[...], jnp.zeros((1, 128 - units), F32)], axis=1)
        own_row = jnp.where(parity == 0, own_row, pltpu.roll(own_row, units, 1))
        ow_all[pl.ds(me_d, 1)] = jnp.broadcast_to(own_row, (8, 128))[None]
        keep_own(snd1, rcv1)

    with jax.named_scope("barrier_wait"):
        pl.semaphore_wait(barrier, n_exp - 1 + n_dp - 1)

    far = n_dp // 2
    near = n_dp - 1 - far

    def hop(chain, step):
        buf, rows, to_right, steps, sem = chain
        owner = lax.rem(me_d + (n_dp - step if to_right else step), n_dp)
        place = buf.at[owner, rows]
        return remote(
            place, place, ring_send.at[sem], ring_recv.at[sem, step], "dp", right if to_right else left
        )

    def came(chain, step):
        buf, rows, to_right, steps, sem = chain
        owner = lax.rem(me_d + (n_dp - 1 - step if to_right else step + 1), n_dp)
        place = buf.at[owner, rows]
        remote(
            place, place, ring_send.at[sem], ring_recv.at[sem, step], "dp", right if to_right else left
        ).wait_recv()

    def ring_start(chains):
        for chain in chains:
            hop(chain, 0).start()

    def ring_step(chains, step, each):
        for chain in chains:
            steps = chain[3]

            @pl.when(step < steps)
            def _(chain=chain, steps=steps):
                came(chain, step)

                @pl.when(step + 1 < steps)
                def _():
                    hop(chain, step + 1).start()

                if each is not None:
                    each(chain, step).start()

    def ring_steps(chains, first, last, each=None):
        def body(step, carry):
            ring_step(chains, step, each)
            return carry

        if first < last:
            lax.fori_loop(first, last, body, 0)

    def ring_drain(chains):
        for buf, rows, to_right, steps, sem in chains:
            place = buf.at[pl.ds(0, steps), rows]
            remote(place, place, ring_send.at[sem], ring_recv.at[sem, 0], "dp", right).wait_send()

    upper = pl.ds(0, units // 2)
    lower = pl.ds(units // 2, units // 2)
    weight_chains = [
        (wide_all, upper, True, far, 0),
        (wide_all, upper, False, near, 1),
        (wide_all, lower, True, near, 2),
        (wide_all, lower, False, far, 3),
        (rest_all, upper, True, far, 4),
        (rest_all, upper, False, near, 5),
        (rest_all, lower, True, near, 6),
        (rest_all, lower, False, far, 7),
    ]
    core = lax.rem(me_e, 2)
    twin = me_e + 1 - 2 * core
    quarter = units // 4

    def head_rows(side, part):
        return pl.ds(pl.multiple_of(side * 2 * quarter + part * quarter, 16), quarter)

    def head_half(side):
        return [
            (head_all, head_rows(side, 0), True, far, 8),
            (head_all, head_rows(side, 0), False, near, 9),
            (head_all, head_rows(side, 1), True, near, 10),
            (head_all, head_rows(side, 1), False, far, 11),
        ]

    head_chains = head_half(core)

    def hand_over(chain, step):
        buf, rows, to_right, steps, sem = chain
        owner = lax.rem(me_d + (n_dp - 1 - step if to_right else step + 1), n_dp)
        place = buf.at[owner, rows]
        return remote(place, place, twin_send.at[sem - 8], twin_recv.at[sem - 8], "expert", twin)

    def twins(chains, do):
        for buf, rows, to_right, steps, sem in chains:
            place = buf.at[pl.ds(0, steps), rows]
            do(remote(place, place, twin_send.at[sem - 8], twin_recv.at[sem - 8], "expert", twin))

    pooled_chains = [
        (pooled_all, pl.ds(0, cands), True, far, 20),
        (pooled_all, pl.ds(0, cands), False, near, 21),
    ]

    def push(n, src, dst, p):
        return remote(src, dst.at[me_d], dp_send.at[n], dp_recv.at[n], "dp", p)

    def pushed(n, dst):
        peers = pl.ds(0, n_dp - 1)
        return remote(dst.at[peers], dst.at[peers], dp_send.at[n], dp_recv.at[n], "dp", right)

    with jax.named_scope("dispatch_send"):
        ring_start(weight_chains)
        for g in range(groups):
            send_group(0, snd1, rcv1, g)
        dp_peers(lambda p: push(0, ow_all.at[me_d], ow_all, p).start())

    with jax.named_scope("mix_tables"):
        weight_high, weight_low = split(weight_t)

        def spread(part, hot, rows):
            wide = jnp.broadcast_to(part.astype(F32)[:, None, :], (n_exp, rows, toks))
            return hot[...].astype(F32) * wide.reshape(n_exp * rows, toks)

        def both(hot, rows):
            return jnp.concatenate(
                [spread(weight_high, hot, rows), spread(weight_low, hot, rows)], axis=1
            )

        table = both(hot_main, MAIN)
        mix_main[...] = table.astype(BF16)
        mix_main_t[...] = jnp.transpose(table).astype(BF16)
        table = both(hot_over, OVER)
        mix_over[...] = table.astype(BF16)
        mix_over_t[...] = jnp.transpose(table).astype(BF16)

    with jax.named_scope("weight_ring"):
        head_at = max(0, min(3, far - 1))
        ring_steps(weight_chains, 0, far - 1 - head_at)
        ring_start(head_chains)
        ring_steps(weight_chains, far - 1 - head_at, far - head_at)

        def both_steps(k, carry):
            ring_step(weight_chains, k + (far - head_at), None)
            ring_step(head_chains, k, hand_over)
            return carry

        lax.fori_loop(0, head_at, both_steps, 0)

    with jax.named_scope("dispatch_wait"):
        exchanged(0, snd1, rcv1).wait_recv()

    with jax.named_scope("expert_forward"):
        if head_at < far:
            ring_step(head_chains, head_at, hand_over)
            head_at += 1
        down_full[:, 0:rest] = rest_all[...].reshape(width, rest)
        down_full[:, rest:lanes] = wide_all[:, :, rest:lanes].reshape(width, lanes - rest)

        def no_column(rows):
            lane = iota((rows, lanes), 1)
            return (lane >= rest) & (lane < rest + spare)

        def forward(g):
            main, over = unpack(rcv1, g)
            rows = pl.ds(g * g_rows, g_rows)
            x = jnp.concatenate([main, over], axis=0)
            x_all[rows, :] = x
            natural = dot(x, wide_all[...].reshape(width, lanes))
            pre_act = jnp.where(no_column(g_rows), 0.0, pltpu.roll(natural, lanes - spare, 1))
            pre[rows, :] = pre_act
            activated = (pre_act * jax.nn.sigmoid(pre_act)).astype(BF16)
            act[rows, :] = activated
            out = dot(activated, down_full[...], 1, 1)
            pack(snd2, g, out[0:g_main], out[g_main:g_rows])
            send_group(1, snd2, rcv2, g)

        for g in range(groups):
            forward(g)
            if head_at < far:
                ring_step(head_chains, head_at, hand_over)
                head_at += 1
        keep_own(snd2, rcv2)

    with jax.named_scope("head_ring"):
        ring_steps(head_chains, head_at, far, hand_over)
        twins(head_half(1 - core), lambda copy: copy.wait_recv())

    with jax.named_scope("slope"):

        def slope(g, carry):
            rows = pl.ds(pl.multiple_of(g * (g_rows // 4), 16), g_rows // 4)
            pre_act = pre[rows, :]
            sigmoid = jax.nn.sigmoid(pre_act)
            slope_of = sigmoid * (1.0 + pre_act * (1.0 - sigmoid))
            pre[rows, :] = jnp.where(no_column(g_rows // 4), 0.0, slope_of)
            return carry

        lax.fori_loop(0, groups * 4, slope, 0)
        pool_row = pool[...].astype(F32)
        member_t = jnp.where(iota((cands, toks), 0).astype(F32) == pool_row, 1.0, 0.0)
        counts = jnp.sum(member_t, axis=1, keepdims=True)
        pool_column = column(pool_row, toks)
        member = jnp.where(iota((toks, cands), 1).astype(F32) == pool_column, 1.0, 0.0).astype(BF16)
        member_t = member_t.astype(BF16)
        list_hot = jnp.where(
            iota((cands, 128), 1).astype(F32) == column(lists[...].astype(F32), cands), 1.0, 0.0
        )
        rank_hot = jnp.where(
            iota((cands, RANKS), 1).astype(F32) == column(ranks[...].astype(F32), cands), 1.0, 0.0
        )
        alpha_of = jnp.sum(rank_hot * alpha[...], axis=1, keepdims=True)
        beta_of = jnp.sum(rank_hot * beta[...], axis=1, keepdims=True)
        corrected = (column(clicks[...].astype(F32), cands) - beta_of) / alpha_of
        pushed(0, ow_all).wait_recv()
        ow_row = jnp.concatenate(
            [(ow_all[2 * k] + ow_all[2 * k + 1])[0:1] for k in range(hidden // 128)], axis=1
        )

    with jax.named_scope("return_wait"):
        exchanged(1, snd2, rcv2).wait_recv()

    with jax.named_scope("mix"):
        stacked = jnp.zeros((2 * toks, width), F32)
        for g in range(groups):
            main, over = unpack(rcv2, g)
            stacked = stacked + dot(mix_main_t[:, g * g_main : (g + 1) * g_main], main)
            stacked = stacked + dot(mix_over_t[:, g * g_over : (g + 1) * g_over], over)
        mixed = tok[...].astype(F32) + (stacked[0:toks] + stacked[toks : 2 * toks])
        inv_rms = lax.rsqrt(jnp.mean(mixed * mixed, axis=1, keepdims=True) + 1e-06)
        normed = mixed * inv_rms
        normed_high, normed_low = split(normed)
        pooled_sum = dot(member_t, normed_high) + dot(member_t, normed_low)
        pooled = (pooled_sum / counts).astype(BF16)
        pooled_all[pl.ds(me_d, 1)] = pooled.reshape(1, cands, width)
        ring_start(pooled_chains)
    with jax.named_scope("head_forward"):
        head_act = jnp.tanh(dot(pooled, head_all[...].reshape(hidden, width), 1, 1))
        scores = jnp.sum(head_act * ow_row, axis=1, keepdims=True)
        exp_scores = jnp.exp(scores)
        tile_row = iota((8, 128), 0)
        terms = jnp.zeros((8, 128), F32)
        for k, value in enumerate((exp_scores, corrected, corrected * scores)):
            terms = jnp.where(tile_row == k, jnp.sum(value * list_hot, axis=0, keepdims=True), terms)
        totals[pl.ds(me_d, 1)] = terms.reshape(1, 8, 128)
    with jax.named_scope("totals"):
        dp_peers(lambda p: push(1, totals.at[me_d], totals, p).start())
        pooled_at = min(2, far)
        ring_steps(pooled_chains, 0, pooled_at)
        pushed(1, totals).wait_recv()
    with jax.named_scope("head_backward"):
        total = jnp.sum(totals[...], axis=0)
        in_list = iota((1, 128), 1) < LISTS
        exp_total = jnp.where(in_list, total[0:1], 1.0)
        click_total = jnp.where(in_list, total[1:2], 0.0)
        cross_total = jnp.where(in_list, total[2:3], 0.0)
        loss[...] = jnp.sum(click_total * jnp.log(exp_total) - cross_total, axis=1, keepdims=True)
        ratio = jnp.sum(list_hot * (click_total / exp_total), axis=1, keepdims=True)
        cand_grad = ratio * exp_scores - corrected
        hid_grad = (cand_grad * ow_row * (1.0 - head_act * head_act)).astype(BF16)
        pooled_grad = dot(hid_grad, head_all[...].reshape(hidden, width)) / counts
        grad_high, grad_low = split(pooled_grad)
        normed_grad = dot(member, grad_high) + dot(member, grad_low)
        mixed_grad = inv_rms * (normed_grad - normed * jnp.mean(normed_grad * normed, axis=1, keepdims=True))
        once = mixed_grad.astype(BF16)
        twice = jnp.concatenate([once, once], axis=0)
    with jax.named_scope("grad_send"):
        for g in range(groups):
            pack(
                snd3,
                g,
                dot(mix_main[g * g_main : (g + 1) * g_main, :], twice),
                dot(mix_over[g * g_over : (g + 1) * g_over, :], twice),
            )
            send_group(2, snd3, rcv3, g)
        keep_own(snd3, rcv3)

        out_term = jnp.sum(cand_grad * head_act, axis=0, keepdims=True)
        for k in range(hidden // 128):
            hid_snd[k] = hid_grad[:, k * 128 : (k + 1) * 128]
            out_snd[k] = jnp.broadcast_to(out_term[:, k * 128 : (k + 1) * 128], (8, 128))
        hid_rcv[pl.ds(me_d, 1)] = hid_snd[pl.ds(me_d // 2, 1)]
        out_rcv[pl.ds(me_d, 1)] = out_snd[pl.ds(me_d // 2, 1)]

        def send_terms(p):
            push(2, hid_snd.at[p // 2], hid_rcv, p).start()
            push(3, out_snd.at[p // 2], out_rcv, p).start()

        dp_peers(send_terms)

    with jax.named_scope("pooled_ring"):
        ring_steps(pooled_chains, pooled_at, far)

    with jax.named_scope("grad_wait"):
        exchanged(2, snd3, rcv3).wait_recv()

    tile = min(256, width)
    blocks = tile // units

    def down_part(f, carry):
        part = dot(g_all[:, pl.ds(pl.multiple_of(f * tile, 128), tile)], act[...], 0, 0)
        place = pl.ds(f * blocks, blocks)
        down_sum[place] = part[:, 0:rest].astype(BF16).reshape(blocks, units, rest)
        up_sum[place, :, rest:lanes] = part[:, rest:lanes].astype(BF16).reshape(blocks, units, lanes - rest)
        return carry

    def up_part(f, carry):
        part = dot(x_all[:, pl.ds(pl.multiple_of(f * tile, 128), tile)], pre_grad[...], 0, 0)
        place = pl.ds(f * blocks, blocks)
        up_sum[place, :, 0:rest] = part[:, 0:rest].astype(BF16).reshape(blocks, units, rest)
        below = up_sum[place, :, rest:lanes].astype(F32).reshape(tile, lanes - rest)
        last = jnp.where(iota(below.shape, 1) < spare, pltpu.roll(below, spare, 1), part[:, rest:lanes])
        up_sum[place, :, rest:lanes] = last.astype(BF16).reshape(blocks, units, lanes - rest)
        return carry

    def sum_hop(chain, step):
        own, ring, to_right, steps, sem, slot, rows = chain
        if isinstance(step, int) and step == 0:
            owner = lax.rem(me_d + (steps if to_right else n_dp - steps), n_dp)
            src = own.at[owner, rows]
        else:
            src = ring.at[slot, step - 1, rows]
        return remote(
            src,
            ring.at[slot, step, rows],
            ring_send.at[sem],
            ring_recv.at[sem, step],
            "dp",
            right if to_right else left,
        )

    def sum_came(chain, step):
        own, ring, to_right, steps, sem, slot, rows = chain
        place = ring.at[slot, step, rows]
        remote(
            place, place, ring_send.at[sem], ring_recv.at[sem, step], "dp", right if to_right else left
        ).wait_recv()

    def sum_chains(own, ring, sem):
        return [
            (own, ring, True, far, sem, 0, upper),
            (own, ring, False, near, sem + 1, 1, upper),
            (own, ring, True, near, sem + 2, 0, lower),
            (own, ring, False, far, sem + 3, 1, lower),
        ]

    up_chains = sum_chains(up_sum, up_ring, 12)
    down_chains = sum_chains(down_sum, down_ring, 16)

    with jax.named_scope("down_term"):

        def gather(g, carry):
            main, over = unpack(rcv3, g)
            rows = pl.ds(pl.multiple_of(g * g_rows, 16), g_rows)
            g_all[rows, :] = jnp.concatenate([main, over], axis=0)
            return carry

        lax.fori_loop(0, groups, gather, 0)
        lax.fori_loop(0, width // tile, down_part, 0)
        for chain in down_chains:
            sum_hop(chain, 0).start()

    with jax.named_scope("up_term"):

        def backward(g, carry):
            rows = pl.ds(pl.multiple_of(g * g_rows, 16), g_rows)
            act_grad = dot(g_all[rows, :], down_full[...])
            pre_grad[rows, :] = (act_grad * pre[rows, :]).astype(BF16)
            return carry

        lax.fori_loop(0, groups, backward, 0)
        lax.fori_loop(0, width // tile, up_part, 0)
        for chain in up_chains:
            sum_hop(chain, 0).start()

    columns = width // 128
    with jax.named_scope("head_term"):

        pushed(2, hid_rcv).wait_recv()
        pushed(3, out_rcv).wait_recv()
        head_term[...] = dot(
            hid_rcv[...].reshape(n_dp * cands, 128), pooled_all[...].reshape(n_dp * cands, width), 0, 0
        )
        mine = head_term[pl.ds(pl.multiple_of(parity * units, 8), units), :].astype(BF16)
        for q in range(n_exp):
            a, b = q // columns, q % columns
            piece_snd[q] = mine[a * 16 : (a + 1) * 16, b * 128 : (b + 1) * 128]
        piece_rcv[pl.ds(me_e, 1)] = piece_snd[pl.ds(me_e, 1)]
        out_piece[pl.ds(me_e, 1)] = jnp.sum(out_rcv[...], axis=0).reshape(1, 8, 128)

    def piece(p):
        return remote(piece_snd.at[p], piece_rcv.at[me_e], exp_send.at[0], exp_recv.at[0], "expert", p)

    def out_push(p):
        return remote(out_piece.at[me_e], out_piece.at[me_e], exp_send.at[1], exp_recv.at[1], "expert", p)

    def whole_push(p):
        return remote(whole_piece.at[me_e], whole_piece.at[me_e], exp_send.at[2], exp_recv.at[2], "expert", p)

    def got(n, ref):
        peers = pl.ds(0, n_exp - 1)
        return remote(ref.at[peers], ref.at[peers], exp_send.at[n], exp_recv.at[n], "expert", next_e)

    def send_pieces(p):
        piece(p).start()
        out_push(p).start()

    expert_peers(send_pieces)

    def sum_steps(first, last):
        def body(step, carry):
            for chain in down_chains + up_chains:
                steps = chain[3]

                @pl.when(step + 1 < steps)
                def _(chain=chain):
                    own, ring, to_right, steps, sem, slot, rows = chain
                    sum_came(chain, step)
                    owner = lax.rem(
                        me_d + (steps - 1 - step if to_right else n_dp - (steps - 1) + step), n_dp
                    )
                    total = ring[slot, pl.ds(step, 1), rows].astype(F32) + own[pl.ds(owner, 1), rows].astype(F32)
                    ring[slot, pl.ds(step, 1), rows] = total.astype(BF16)
                    sum_hop(chain, step + 1).start()

            return carry

        lax.fori_loop(first, last, body, 0)

    with jax.named_scope("sum_ring_first"):
        middle = min(3, far - 1)
        sum_steps(0, middle)

    with jax.named_scope("head_pieces"):
        got(0, piece_rcv).wait_recv()
        whole_piece[pl.ds(me_e, 1)] = jnp.sum(piece_rcv[...].astype(F32), axis=0).reshape(1, 16, 128)
        expert_peers(lambda p: whole_push(p).start())

    with jax.named_scope("sum_ring_last"):
        sum_steps(middle, far - 1)

    with jax.named_scope("head_out"):
        got(1, out_piece).wait_recv()
        out_all = jnp.sum(out_piece[...], axis=0)[0:1]
        out_pair = jnp.where(parity == 0, out_all, pltpu.roll(out_all, 128 - units, 1))
        grad_out[...] = out_pair[:, 0:units]
        got(2, whole_piece).wait_recv()
        for q in range(n_exp):
            a, b = q // columns, q % columns
            grad_head[a * 16 : (a + 1) * 16, b * 128 : (b + 1) * 128] = whole_piece[q]

    with jax.named_scope("sum_end"):
        sums = []
        for chains in (down_chains, up_chains):
            halves = []
            for pair in (chains[0:2], chains[2:4]):
                total = 0.0
                for chain in pair:
                    own, ring, to_right, steps, sem, slot, rows = chain
                    sum_came(chain, steps - 1)
                    total = total + ring[slot, steps - 1, rows].astype(F32)
                halves.append(total + own[pl.ds(me_d, 1), rows][0].astype(F32))
            sums.append(jnp.concatenate(halves, axis=0))
        most, wide = sums
        grad_up[...] = pltpu.roll(wide, spare, 1)[:, 0:ff].astype(BF16)[None]
        whole = jnp.concatenate([most, pltpu.roll(wide[:, rest:lanes], spare, 1)], axis=1)
        grad_down[...] = pltpu.roll(whole, spare, 1)[:, 0:ff].astype(BF16)[None]

    with jax.named_scope("drain"):
        exchanged(0, snd1, rcv1).wait_send()
        exchanged(1, snd2, rcv2).wait_send()
        exchanged(2, snd3, rcv3).wait_send()
        for n, ref in enumerate((ow_all, totals, hid_rcv, out_rcv)):
            pushed(n, ref).wait_send()
        for n, ref in enumerate((piece_rcv, out_piece, whole_piece)):
            got(n, ref).wait_send()
        ring_drain(weight_chains + head_chains + pooled_chains)
        twins(head_chains, lambda copy: copy.wait_send())
        for own, ring, to_right, steps, sem, slot, rows in down_chains + up_chains:
            place = ring.at[slot, pl.ds(0, steps), rows]
            remote(place, place, ring_send.at[sem], ring_recv.at[sem, 0], "dp", right).wait_send()


def hand_out(*refs):
    for src, dst in zip(refs[:5], refs[5:]):
        dst[...] = src[...]


def local(
    tokens,
    route_ids,
    route_weights,
    up_weight,
    down_weight,
    head_weight,
    out_weight,
    pool_ids,
    list_ids,
    clicks,
    ranks,
    alpha_table,
    beta_table,
):
    n_dp = lax.axis_size("dp")
    n_exp = lax.axis_size("expert")
    toks, width = tokens.shape
    ff = up_weight.shape[2]
    lanes = -(-ff // 128) * 128
    rest = 2 * ff - lanes
    units = head_weight.shape[0]
    cands = list_ids.shape[1]
    slots = n_exp * (MAIN + OVER)
    wire = pltpu.VMEM((n_exp, MAIN, width + width // 2), BF16)
    steps = n_dp // 2
    pairs = units * n_dp // 128
    vmem = pl.BlockSpec(memory_space=pltpu.VMEM)
    outs = pl.pallas_call(
        functools.partial(kernel, n_dp, n_exp),
        out_shape=(
            jax.ShapeDtypeStruct(up_weight.shape, BF16),
            jax.ShapeDtypeStruct(down_weight.shape, BF16),
            jax.ShapeDtypeStruct(head_weight.shape, F32),
            jax.ShapeDtypeStruct((1, units), F32),
            jax.ShapeDtypeStruct((1, 1), F32),
        ),
        in_specs=[vmem] * 13,
        out_specs=(vmem,) * 5,
        scratch_shapes=[
            wire,
            wire,
            wire,
            wire,
            wire,
            wire,
            pltpu.VMEM((n_exp * MAIN, toks), BF16),
            pltpu.VMEM((n_exp * OVER, toks), BF16),
            pltpu.VMEM((n_exp * MAIN, 2 * toks), BF16),
            pltpu.VMEM((n_exp * OVER, 2 * toks), BF16),
            pltpu.VMEM((2 * toks, n_exp * MAIN), BF16),
            pltpu.VMEM((2 * toks, n_exp * OVER), BF16),
            pltpu.VMEM((slots, width), BF16),
            pltpu.VMEM((slots, width), BF16),
            pltpu.VMEM((slots, lanes), F32),
            pltpu.VMEM((slots, lanes), BF16),
            pltpu.VMEM((slots, lanes), BF16),
            pltpu.VMEM((n_dp, width // n_dp, lanes), BF16),
            pltpu.VMEM((n_dp, width // n_dp, rest), BF16),
            pltpu.VMEM((width, lanes), BF16),
            pltpu.VMEM((n_dp, units, width), BF16),
            pltpu.VMEM((n_dp, 8, 128), F32),
            pltpu.VMEM((n_dp, width // n_dp, lanes), BF16),
            pltpu.VMEM((n_dp, width // n_dp, rest), BF16),
            pltpu.VMEM((2, steps, width // n_dp, lanes), BF16),
            pltpu.VMEM((2, steps, width // n_dp, rest), BF16),
            pltpu.VMEM((n_dp, 8, 128), F32),
            pltpu.VMEM((pairs, cands, 128), BF16),
            pltpu.VMEM((n_dp, cands, 128), BF16),
            pltpu.VMEM((n_dp, cands, width), BF16),
            pltpu.VMEM((pairs, 8, 128), F32),
            pltpu.VMEM((n_dp, 8, 128), F32),
            pltpu.VMEM((128, width), F32),
            pltpu.VMEM((n_exp, 16, 128), BF16),
            pltpu.VMEM((n_exp, 16, 128), BF16),
            pltpu.VMEM((n_exp, 16, 128), F32),
            pltpu.VMEM((n_exp, 8, 128), F32),
            pltpu.SemaphoreType.DMA((3,)),
            pltpu.SemaphoreType.DMA((3,)),
            pltpu.SemaphoreType.DMA((22,)),
            pltpu.SemaphoreType.DMA((22, steps)),
            pltpu.SemaphoreType.DMA((4,)),
            pltpu.SemaphoreType.DMA((4,)),
            pltpu.SemaphoreType.DMA((3,)),
            pltpu.SemaphoreType.DMA((3,)),
            pltpu.SemaphoreType.DMA((4,)),
            pltpu.SemaphoreType.DMA((4,)),
        ],
        compiler_params=pltpu.CompilerParams(
            collective_id=0, has_side_effects=True, vmem_limit_bytes=56 * 1024 * 1024
        ),
    )(
        tokens,
        route_ids.T,
        route_weights.T,
        up_weight,
        down_weight,
        head_weight,
        out_weight.reshape(1, units),
        pool_ids,
        list_ids,
        clicks,
        ranks,
        alpha_table.reshape(1, RANKS),
        beta_table.reshape(1, RANKS),
    )
    grad_up, grad_down, grad_head, grad_out, list_loss = pl.pallas_call(
        hand_out,
        out_shape=[jax.ShapeDtypeStruct(o.shape, o.dtype) for o in outs],
        in_specs=[vmem] * 5,
        out_specs=[vmem] * 5,
    )(*outs)
    return grad_up, grad_down, grad_head, grad_out.reshape(units), list_loss.reshape(1)


def solution(mesh):
    return jax.shard_map(
        local,
        mesh=mesh,
        in_specs=(
            P(("dp", "expert"), None),
            P(("dp", "expert"), None),
            P(("dp", "expert"), None),
            P("expert", "dp", None),
            P("expert", "dp", None),
            P("dp", None),
            P("dp"),
            P(("dp", "expert"), None),
            P(("dp", "expert"), None),
            P(("dp", "expert"), None),
            P(("dp", "expert"), None),
            P(),
            P(),
        ),
        out_specs=(
            P("expert", "dp", None),
            P("expert", "dp", None),
            P("dp", None),
            P("dp"),
            P("expert"),
        ),
        check_vma=False,
    )
```

```python
import functools

import jax
import jax.numpy as jnp
from jax import lax
from jax.experimental import pallas as pl
from jax.experimental.pallas import tpu as pltpu
from jax.sharding import PartitionSpec as P

LISTS = 8
RANKS = 32
MAIN = 16
OVER = 8
F32 = jnp.float32
BF16 = jnp.bfloat16
MESH = pl.DeviceIdType.MESH


def dot(a, b, ca=1, cb=0):
    return lax.dot_general(a, b, (((ca,), (cb,)), ((), ())), preferred_element_type=F32)


def iota(shape, dim):
    return lax.broadcasted_iota(jnp.int32, shape, dim)


def column(row, size):
    diagonal = iota((size, size), 0) == iota((size, size), 1)
    return jnp.sum(jnp.where(diagonal, jnp.broadcast_to(row, (size, size)), 0.0), axis=1, keepdims=True)


def split(value):
    high = value.astype(BF16)
    return high, (value - high.astype(F32)).astype(BF16)


def kernel(
    n_dp,
    n_exp,
    tok,
    ids,
    wts,
    up,
    down,
    head,
    out_w,
    pool,
    lists,
    clicks,
    ranks,
    alpha,
    beta,
    grad_up,
    grad_down,
    grad_head,
    grad_out,
    loss,
    snd1,
    rcv1,
    snd2,
    rcv2,
    snd3,
    rcv3,
    hot_main,
    hot_over,
    mix_main,
    mix_over,
    mix_main_t,
    mix_over_t,
    x_all,
    g_all,
    pre,
    act,
    pre_grad,
    wide_all,
    rest_all,
    down_full,
    head_all,
    ow_all,
    up_sum,
    down_sum,
    up_ring,
    down_ring,
    totals,
    hid_snd,
    hid_rcv,
    pooled_all,
    out_snd,
    out_rcv,
    head_term,
    piece_snd,
    piece_rcv,
    whole_piece,
    out_piece,
    a2a_send,
    a2a_recv,
    ring_send,
    ring_recv,
    dp_send,
    dp_recv,
    exp_send,
    exp_recv,
    twin_send,
    twin_recv,
):
    toks, width = tok.shape
    top = ids.shape[0]
    ff = up.shape[2]
    lanes = wide_all.shape[2]
    spare = lanes - ff
    rest = rest_all.shape[2]
    half = width // 2
    cands = lists.shape[1]
    units = head.shape[0]
    hidden = units * n_dp
    group = min(16, n_exp)
    groups = n_exp // group
    g_main, g_over = group * MAIN, group * OVER
    g_rows = g_main + g_over
    me_d = lax.axis_index("dp")
    me_e = lax.axis_index("expert")
    right = lax.rem(me_d + 1, n_dp)
    left = lax.rem(me_d + n_dp - 1, n_dp)

    def expert_peers(do):
        def body(k, carry):
            do(lax.rem(me_e + k, n_exp))
            return carry

        lax.fori_loop(1, n_exp, body, 0)

    def dp_peers(do):
        def body(k, carry):
            away = n_dp // 2 + ((k + 1) // 2) * (1 - 2 * lax.rem(k, 2))
            do(lax.rem(me_d + away, n_dp))
            return carry

        lax.fori_loop(0, n_dp - 1, body, 0)

    def remote(src, dst, send, recv, axis, peer):
        return pltpu.make_async_remote_copy(
            src_ref=src,
            dst_ref=dst,
            send_sem=send,
            recv_sem=recv,
            device_id={axis: peer},
            device_id_type=MESH,
        )

    def exchange(n, src, dst, p):
        return remote(src.at[p], dst.at[me_e], a2a_send.at[n], a2a_recv.at[n], "expert", p)

    next_e = lax.rem(me_e + 1, n_exp)

    def exchanged(n, src, dst):
        peers = pl.ds(0, n_exp - 1)
        return remote(src.at[peers], dst.at[peers], a2a_send.at[n], a2a_recv.at[n], "expert", next_e)

    def send_group(n, src, dst, g):
        def body(k, carry):
            p = g * group + lax.rem(me_e + k, group)

            @pl.when(p != me_e)
            def _():
                exchange(n, src, dst, p).start()

            return carry

        lax.fori_loop(0, group, body, 0)

    def keep_own(src, dst):
        dst[pl.ds(me_e, 1)] = src[pl.ds(me_e, 1)]

    def pack(dst, g, main, over):
        peers = pl.ds(g * group, group)
        dst[peers, :, 0:width] = main.astype(BF16).reshape(group, MAIN, width)
        low = over[:, 0:half].reshape(group, OVER, half)
        high = over[:, half:width].reshape(group, OVER, half)
        dst[peers, :, width : width + half] = jnp.concatenate([low, high], axis=1).astype(BF16)

    def unpack(src, g):
        peers = pl.ds(g * group, group)
        main = src[peers, :, 0:width].reshape(g_main, width)
        both = src[peers, :, width : width + half].astype(F32)
        low = both[:, 0:OVER, :].reshape(g_over, half)
        high = both[:, OVER : 2 * OVER, :].reshape(g_over, half)
        return main, jnp.concatenate([low, high], axis=1).astype(BF16)

    with jax.named_scope("greet"):
        barrier = pltpu.get_barrier_semaphore()
        expert_peers(
            lambda p: pl.semaphore_signal(barrier, inc=1, device_id={"expert": p}, device_id_type=MESH)
        )
        dp_peers(lambda p: pl.semaphore_signal(barrier, inc=1, device_id={"dp": p}, device_id_type=MESH))

    with jax.named_scope("slots"):
        pad = jnp.zeros((up.shape[1], spare), F32)
        turned = pltpu.roll(jnp.concatenate([down[0].astype(F32), pad], axis=1), lanes - spare, 1)
        up_wide = jnp.concatenate([up[0].astype(F32), pad], axis=1)
        own_wide = jnp.where(iota((up.shape[1], lanes), 1) < ff, up_wide, turned)
        wide_all[pl.ds(me_d, 1)] = own_wide.astype(BF16)[None]
        rest_all[pl.ds(me_d, 1)] = turned[:, 0:rest].astype(BF16)[None]
        head_all[pl.ds(me_d, 1)] = head[...].reshape(1, units, width)
        expert = iota((n_exp, toks), 0)
        named_t = jnp.zeros((n_exp, toks), F32)
        weight_t = jnp.zeros((n_exp, toks), F32)
        for k in range(top):
            hit = ids[k : k + 1, :] == expert
            named_t = jnp.where(hit, 1.0, named_t)
            weight_t = jnp.where(hit, wts[k : k + 1, :], weight_t)
        earlier = jnp.where(iota((toks, toks), 0) < iota((toks, toks), 1), 1.0, 0.0).astype(BF16)
        slot_t = jnp.where(named_t > 0.5, dot(named_t.astype(BF16), earlier), -1.0)

        def one_hot(first, rows):
            slot = (iota((n_exp, rows, toks), 1) + first).astype(F32)
            return jnp.where(slot_t[:, None, :] == slot, 1.0, 0.0).reshape(n_exp * rows, toks)

        hot_main[...] = one_hot(0, MAIN).astype(BF16)
        hot_over[...] = one_hot(MAIN, OVER).astype(BF16)

        def dispatch(g, carry):
            pack(
                snd1,
                g,
                dot(hot_main[pl.ds(g * g_main, g_main), :], tok[...]),
                dot(hot_over[pl.ds(g * g_over, g_over), :], tok[...]),
            )
            return carry

        lax.fori_loop(0, groups, dispatch, 0)
        parity = lax.rem(me_d, 2)
        own_row = jnp.concatenate([out_w[...], jnp.zeros((1, 128 - units), F32)], axis=1)
        own_row = jnp.where(parity == 0, own_row, pltpu.roll(own_row, units, 1))
        ow_all[pl.ds(me_d, 1)] = jnp.broadcast_to(own_row, (8, 128))[None]
        keep_own(snd1, rcv1)

    with jax.named_scope("barrier_wait"):
        pl.semaphore_wait(barrier, n_exp - 1 + n_dp - 1)

    far = n_dp // 2
    near = n_dp - 1 - far

    def hop(chain, step):
        buf, rows, to_right, steps, sem = chain
        owner = lax.rem(me_d + (n_dp - step if to_right else step), n_dp)
        place = buf.at[owner, rows]
        return remote(
            place, place, ring_send.at[sem], ring_recv.at[sem, step], "dp", right if to_right else left
        )

    def came(chain, step):
        buf, rows, to_right, steps, sem = chain
        owner = lax.rem(me_d + (n_dp - 1 - step if to_right else step + 1), n_dp)
        place = buf.at[owner, rows]
        remote(
            place, place, ring_send.at[sem], ring_recv.at[sem, step], "dp", right if to_right else left
        ).wait_recv()

    def ring_start(chains):
        for chain in chains:
            hop(chain, 0).start()

    def ring_step(chains, step, each):
        for chain in chains:
            steps = chain[3]

            @pl.when(step < steps)
            def _(chain=chain, steps=steps):
                came(chain, step)

                @pl.when(step + 1 < steps)
                def _():
                    hop(chain, step + 1).start()

                if each is not None:
                    each(chain, step).start()

    def ring_steps(chains, first, last, each=None):
        def body(step, carry):
            ring_step(chains, step, each)
            return carry

        if first < last:
            lax.fori_loop(first, last, body, 0)

    def ring_drain(chains):
        for buf, rows, to_right, steps, sem in chains:
            place = buf.at[pl.ds(0, steps), rows]
            remote(place, place, ring_send.at[sem], ring_recv.at[sem, 0], "dp", right).wait_send()

    upper = pl.ds(0, units // 2)
    lower = pl.ds(units // 2, units // 2)
    weight_chains = [
        (wide_all, upper, True, far, 0),
        (wide_all, upper, False, near, 1),
        (wide_all, lower, True, near, 2),
        (wide_all, lower, False, far, 3),
        (rest_all, upper, True, far, 4),
        (rest_all, upper, False, near, 5),
        (rest_all, lower, True, near, 6),
        (rest_all, lower, False, far, 7),
    ]
    core = lax.rem(me_e, 2)
    twin = me_e + 1 - 2 * core
    quarter = units // 4

    def head_rows(side, part):
        return pl.ds(pl.multiple_of(side * 2 * quarter + part * quarter, 16), quarter)

    def head_half(side):
        return [
            (head_all, head_rows(side, 0), True, far, 8),
            (head_all, head_rows(side, 0), False, near, 9),
            (head_all, head_rows(side, 1), True, near, 10),
            (head_all, head_rows(side, 1), False, far, 11),
        ]

    head_chains = head_half(core)

    def hand_over(chain, step):
        buf, rows, to_right, steps, sem = chain
        owner = lax.rem(me_d + (n_dp - 1 - step if to_right else step + 1), n_dp)
        place = buf.at[owner, rows]
        return remote(place, place, twin_send.at[sem - 8], twin_recv.at[sem - 8], "expert", twin)

    def twins(chains, do):
        for buf, rows, to_right, steps, sem in chains:
            place = buf.at[pl.ds(0, steps), rows]
            do(remote(place, place, twin_send.at[sem - 8], twin_recv.at[sem - 8], "expert", twin))

    pooled_chains = [
        (pooled_all, pl.ds(0, cands), True, far, 20),
        (pooled_all, pl.ds(0, cands), False, near, 21),
    ]

    def push(n, src, dst, p):
        return remote(src, dst.at[me_d], dp_send.at[n], dp_recv.at[n], "dp", p)

    def pushed(n, dst):
        peers = pl.ds(0, n_dp - 1)
        return remote(dst.at[peers], dst.at[peers], dp_send.at[n], dp_recv.at[n], "dp", right)

    with jax.named_scope("dispatch_send"):
        ring_start(weight_chains)
        for g in range(groups):
            send_group(0, snd1, rcv1, g)
        dp_peers(lambda p: push(0, ow_all.at[me_d], ow_all, p).start())

    with jax.named_scope("mix_tables"):
        weight_high, weight_low = split(weight_t)

        def spread(part, hot, rows):
            wide = jnp.broadcast_to(part.astype(F32)[:, None, :], (n_exp, rows, toks))
            return hot[...].astype(F32) * wide.reshape(n_exp * rows, toks)

        def both(hot, rows):
            return jnp.concatenate(
                [spread(weight_high, hot, rows), spread(weight_low, hot, rows)], axis=1
            )

        table = both(hot_main, MAIN)
        mix_main[...] = table.astype(BF16)
        mix_main_t[...] = jnp.transpose(table).astype(BF16)
        table = both(hot_over, OVER)
        mix_over[...] = table.astype(BF16)
        mix_over_t[...] = jnp.transpose(table).astype(BF16)

    with jax.named_scope("weight_ring"):
        head_at = max(0, min(3, far - 1))
        ring_steps(weight_chains, 0, far - 1 - head_at)
        ring_start(head_chains)
        ring_steps(weight_chains, far - 1 - head_at, far - head_at)

        def both_steps(k, carry):
            ring_step(weight_chains, k + (far - head_at), None)
            ring_step(head_chains, k, hand_over)
            return carry

        lax.fori_loop(0, head_at, both_steps, 0)

    with jax.named_scope("dispatch_wait"):
        exchanged(0, snd1, rcv1).wait_recv()

    with jax.named_scope("expert_forward"):
        if head_at < far:
            ring_step(head_chains, head_at, hand_over)
            head_at += 1
        down_full[:, 0:rest] = rest_all[...].reshape(width, rest)
        down_full[:, rest:lanes] = wide_all[:, :, rest:lanes].reshape(width, lanes - rest)

        def no_column(rows):
            lane = iota((rows, lanes), 1)
            return (lane >= rest) & (lane < rest + spare)

        def forward(g):
            main, over = unpack(rcv1, g)
            rows = pl.ds(g * g_rows, g_rows)
            x = jnp.concatenate([main, over], axis=0)
            x_all[rows, :] = x
            natural = dot(x, wide_all[...].reshape(width, lanes))
            pre_act = jnp.where(no_column(g_rows), 0.0, pltpu.roll(natural, lanes - spare, 1))
            pre[rows, :] = pre_act
            activated = (pre_act * jax.nn.sigmoid(pre_act)).astype(BF16)
            act[rows, :] = activated
            out = dot(activated, down_full[...], 1, 1)
            pack(snd2, g, out[0:g_main], out[g_main:g_rows])
            send_group(1, snd2, rcv2, g)

        for g in range(groups):
            forward(g)
            if head_at < far:
                ring_step(head_chains, head_at, hand_over)
                head_at += 1
        keep_own(snd2, rcv2)

    with jax.named_scope("head_ring"):
        ring_steps(head_chains, head_at, far, hand_over)
        twins(head_half(1 - core), lambda copy: copy.wait_recv())

    with jax.named_scope("slope"):

        def slope(g, carry):
            rows = pl.ds(pl.multiple_of(g * (g_rows // 4), 16), g_rows // 4)
            pre_act = pre[rows, :]
            sigmoid = jax.nn.sigmoid(pre_act)
            slope_of = sigmoid * (1.0 + pre_act * (1.0 - sigmoid))
            pre[rows, :] = jnp.where(no_column(g_rows // 4), 0.0, slope_of)
            return carry

        lax.fori_loop(0, groups * 4, slope, 0)
        pool_row = pool[...].astype(F32)
        member_t = jnp.where(iota((cands, toks), 0).astype(F32) == pool_row, 1.0, 0.0)
        counts = jnp.sum(member_t, axis=1, keepdims=True)
        pool_column = column(pool_row, toks)
        member = jnp.where(iota((toks, cands), 1).astype(F32) == pool_column, 1.0, 0.0).astype(BF16)
        member_t = member_t.astype(BF16)
        list_hot = jnp.where(
            iota((cands, 128), 1).astype(F32) == column(lists[...].astype(F32), cands), 1.0, 0.0
        )
        rank_hot = jnp.where(
            iota((cands, RANKS), 1).astype(F32) == column(ranks[...].astype(F32), cands), 1.0, 0.0
        )
        alpha_of = jnp.sum(rank_hot * alpha[...], axis=1, keepdims=True)
        beta_of = jnp.sum(rank_hot * beta[...], axis=1, keepdims=True)
        corrected = (column(clicks[...].astype(F32), cands) - beta_of) / alpha_of
        pushed(0, ow_all).wait_recv()
        ow_row = jnp.concatenate(
            [(ow_all[2 * k] + ow_all[2 * k + 1])[0:1] for k in range(hidden // 128)], axis=1
        )

    with jax.named_scope("return_wait"):
        exchanged(1, snd2, rcv2).wait_recv()

    with jax.named_scope("mix"):
        stacked = jnp.zeros((2 * toks, width), F32)
        for g in range(groups):
            main, over = unpack(rcv2, g)
            stacked = stacked + dot(mix_main_t[:, g * g_main : (g + 1) * g_main], main)
            stacked = stacked + dot(mix_over_t[:, g * g_over : (g + 1) * g_over], over)
        mixed = tok[...].astype(F32) + (stacked[0:toks] + stacked[toks : 2 * toks])
        inv_rms = lax.rsqrt(jnp.mean(mixed * mixed, axis=1, keepdims=True) + 1e-06)
        normed = mixed * inv_rms
        normed_high, normed_low = split(normed)
        pooled_sum = dot(member_t, normed_high) + dot(member_t, normed_low)
        pooled = (pooled_sum / counts).astype(BF16)
        pooled_all[pl.ds(me_d, 1)] = pooled.reshape(1, cands, width)
        ring_start(pooled_chains)
    with jax.named_scope("head_forward"):
        head_act = jnp.tanh(dot(pooled, head_all[...].reshape(hidden, width), 1, 1))
        scores = jnp.sum(head_act * ow_row, axis=1, keepdims=True)
        exp_scores = jnp.exp(scores)
        tile_row = iota((8, 128), 0)
        terms = jnp.zeros((8, 128), F32)
        for k, value in enumerate((exp_scores, corrected, corrected * scores)):
            terms = jnp.where(tile_row == k, jnp.sum(value * list_hot, axis=0, keepdims=True), terms)
        totals[pl.ds(me_d, 1)] = terms.reshape(1, 8, 128)
    with jax.named_scope("totals"):
        dp_peers(lambda p: push(1, totals.at[me_d], totals, p).start())
        pooled_at = min(2, far)
        ring_steps(pooled_chains, 0, pooled_at)
        pushed(1, totals).wait_recv()
    with jax.named_scope("head_backward"):
        total = jnp.sum(totals[...], axis=0)
        in_list = iota((1, 128), 1) < LISTS
        exp_total = jnp.where(in_list, total[0:1], 1.0)
        click_total = jnp.where(in_list, total[1:2], 0.0)
        cross_total = jnp.where(in_list, total[2:3], 0.0)
        loss[...] = jnp.sum(click_total * jnp.log(exp_total) - cross_total, axis=1, keepdims=True)
        ratio = jnp.sum(list_hot * (click_total / exp_total), axis=1, keepdims=True)
        cand_grad = ratio * exp_scores - corrected
        hid_grad = (cand_grad * ow_row * (1.0 - head_act * head_act)).astype(BF16)
        pooled_grad = dot(hid_grad, head_all[...].reshape(hidden, width)) / counts
        grad_high, grad_low = split(pooled_grad)
        normed_grad = dot(member, grad_high) + dot(member, grad_low)
        mixed_grad = inv_rms * (normed_grad - normed * jnp.mean(normed_grad * normed, axis=1, keepdims=True))
        once = mixed_grad.astype(BF16)
        twice = jnp.concatenate([once, once], axis=0)
    with jax.named_scope("grad_send"):
        for g in range(groups):
            pack(
                snd3,
                g,
                dot(mix_main[g * g_main : (g + 1) * g_main, :], twice),
                dot(mix_over[g * g_over : (g + 1) * g_over, :], twice),
            )
            send_group(2, snd3, rcv3, g)
        keep_own(snd3, rcv3)

        out_term = jnp.sum(cand_grad * head_act, axis=0, keepdims=True)
        for k in range(hidden // 128):
            hid_snd[k] = hid_grad[:, k * 128 : (k + 1) * 128]
            out_snd[k] = jnp.broadcast_to(out_term[:, k * 128 : (k + 1) * 128], (8, 128))
        hid_rcv[pl.ds(me_d, 1)] = hid_snd[pl.ds(me_d // 2, 1)]
        out_rcv[pl.ds(me_d, 1)] = out_snd[pl.ds(me_d // 2, 1)]

        def send_terms(p):
            push(2, hid_snd.at[p // 2], hid_rcv, p).start()
            push(3, out_snd.at[p // 2], out_rcv, p).start()

        dp_peers(send_terms)

    with jax.named_scope("pooled_ring"):
        ring_steps(pooled_chains, pooled_at, far)

    with jax.named_scope("grad_wait"):
        exchanged(2, snd3, rcv3).wait_recv()

    tile = min(1024, width)
    blocks = tile // units

    def down_part(f, carry):
        part = dot(g_all[:, pl.ds(pl.multiple_of(f * tile, 128), tile)], act[...], 0, 0)
        place = pl.ds(f * blocks, blocks)
        down_sum[place] = part[:, 0:rest].astype(BF16).reshape(blocks, units, rest)
        up_sum[place, :, rest:lanes] = part[:, rest:lanes].astype(BF16).reshape(blocks, units, lanes - rest)
        return carry

    def up_part(f, carry):
        part = dot(x_all[:, pl.ds(pl.multiple_of(f * tile, 128), tile)], pre_grad[...], 0, 0)
        place = pl.ds(f * blocks, blocks)
        up_sum[place, :, 0:rest] = part[:, 0:rest].astype(BF16).reshape(blocks, units, rest)
        below = up_sum[place, :, rest:lanes].astype(F32).reshape(tile, lanes - rest)
        last = jnp.where(iota(below.shape, 1) < spare, pltpu.roll(below, spare, 1), part[:, rest:lanes])
        up_sum[place, :, rest:lanes] = last.astype(BF16).reshape(blocks, units, lanes - rest)
        return carry

    def sum_hop(chain, step):
        own, ring, to_right, steps, sem, slot, rows = chain
        if isinstance(step, int) and step == 0:
            owner = lax.rem(me_d + (steps if to_right else n_dp - steps), n_dp)
            src = own.at[owner, rows]
        else:
            src = ring.at[slot, step - 1, rows]
        return remote(
            src,
            ring.at[slot, step, rows],
            ring_send.at[sem],
            ring_recv.at[sem, step],
            "dp",
            right if to_right else left,
        )

    def sum_came(chain, step):
        own, ring, to_right, steps, sem, slot, rows = chain
        place = ring.at[slot, step, rows]
        remote(
            place, place, ring_send.at[sem], ring_recv.at[sem, step], "dp", right if to_right else left
        ).wait_recv()

    def sum_chains(own, ring, sem):
        return [
            (own, ring, True, far, sem, 0, upper),
            (own, ring, False, near, sem + 1, 1, upper),
            (own, ring, True, near, sem + 2, 0, lower),
            (own, ring, False, far, sem + 3, 1, lower),
        ]

    up_chains = sum_chains(up_sum, up_ring, 12)
    down_chains = sum_chains(down_sum, down_ring, 16)

    with jax.named_scope("down_term"):

        def gather(g, carry):
            main, over = unpack(rcv3, g)
            rows = pl.ds(pl.multiple_of(g * g_rows, 16), g_rows)
            g_all[rows, :] = jnp.concatenate([main, over], axis=0)
            return carry

        lax.fori_loop(0, groups, gather, 0)
        lax.fori_loop(0, width // tile, down_part, 0)
        for chain in down_chains:
            sum_hop(chain, 0).start()

    with jax.named_scope("up_term"):

        def backward(g, carry):
            rows = pl.ds(pl.multiple_of(g * g_rows, 16), g_rows)
            act_grad = dot(g_all[rows, :], down_full[...])
            pre_grad[rows, :] = (act_grad * pre[rows, :]).astype(BF16)
            return carry

        lax.fori_loop(0, groups, backward, 0)
        lax.fori_loop(0, width // tile, up_part, 0)
        for chain in up_chains:
            sum_hop(chain, 0).start()

    columns = width // 128
    with jax.named_scope("head_term"):

        pushed(2, hid_rcv).wait_recv()
        pushed(3, out_rcv).wait_recv()
        head_term[...] = dot(
            hid_rcv[...].reshape(n_dp * cands, 128), pooled_all[...].reshape(n_dp * cands, width), 0, 0
        )
        mine = head_term[pl.ds(pl.multiple_of(parity * units, 8), units), :].astype(BF16)
        for q in range(n_exp):
            a, b = q // columns, q % columns
            piece_snd[q] = mine[a * 16 : (a + 1) * 16, b * 128 : (b + 1) * 128]
        piece_rcv[pl.ds(me_e, 1)] = piece_snd[pl.ds(me_e, 1)]
        out_piece[pl.ds(me_e, 1)] = jnp.sum(out_rcv[...], axis=0).reshape(1, 8, 128)

    def piece(p):
        return remote(piece_snd.at[p], piece_rcv.at[me_e], exp_send.at[0], exp_recv.at[0], "expert", p)

    def out_push(p):
        return remote(out_piece.at[me_e], out_piece.at[me_e], exp_send.at[1], exp_recv.at[1], "expert", p)

    def whole_push(p):
        return remote(whole_piece.at[me_e], whole_piece.at[me_e], exp_send.at[2], exp_recv.at[2], "expert", p)

    def got(n, ref):
        peers = pl.ds(0, n_exp - 1)
        return remote(ref.at[peers], ref.at[peers], exp_send.at[n], exp_recv.at[n], "expert", next_e)

    def send_pieces(p):
        piece(p).start()
        out_push(p).start()

    expert_peers(send_pieces)

    def sum_steps(first, last):
        def body(step, carry):
            for chain in down_chains + up_chains:
                steps = chain[3]

                @pl.when(step + 1 < steps)
                def _(chain=chain):
                    own, ring, to_right, steps, sem, slot, rows = chain
                    sum_came(chain, step)
                    owner = lax.rem(
                        me_d + (steps - 1 - step if to_right else n_dp - (steps - 1) + step), n_dp
                    )
                    total = ring[slot, pl.ds(step, 1), rows].astype(F32) + own[pl.ds(owner, 1), rows].astype(F32)
                    ring[slot, pl.ds(step, 1), rows] = total.astype(BF16)
                    sum_hop(chain, step + 1).start()

            return carry

        lax.fori_loop(first, last, body, 0)

    with jax.named_scope("sum_ring_first"):
        middle = min(3, far - 1)
        sum_steps(0, middle)

    with jax.named_scope("head_pieces"):
        got(0, piece_rcv).wait_recv()
        whole_piece[pl.ds(me_e, 1)] = jnp.sum(piece_rcv[...].astype(F32), axis=0).reshape(1, 16, 128)
        expert_peers(lambda p: whole_push(p).start())

    with jax.named_scope("sum_ring_last"):
        sum_steps(middle, far - 1)

    with jax.named_scope("head_out"):
        got(1, out_piece).wait_recv()
        out_all = jnp.sum(out_piece[...], axis=0)[0:1]
        out_pair = jnp.where(parity == 0, out_all, pltpu.roll(out_all, 128 - units, 1))
        grad_out[...] = out_pair[:, 0:units]
        got(2, whole_piece).wait_recv()
        for q in range(n_exp):
            a, b = q // columns, q % columns
            grad_head[a * 16 : (a + 1) * 16, b * 128 : (b + 1) * 128] = whole_piece[q]

    with jax.named_scope("sum_end"):
        sums = []
        for chains in (down_chains, up_chains):
            halves = []
            for pair in (chains[0:2], chains[2:4]):
                total = 0.0
                for chain in pair:
                    own, ring, to_right, steps, sem, slot, rows = chain
                    sum_came(chain, steps - 1)
                    total = total + ring[slot, steps - 1, rows].astype(F32)
                halves.append(total + own[pl.ds(me_d, 1), rows][0].astype(F32))
            sums.append(jnp.concatenate(halves, axis=0))
        most, wide = sums
        grad_up[...] = pltpu.roll(wide, spare, 1)[:, 0:ff].astype(BF16)[None]
        whole = jnp.concatenate([most, pltpu.roll(wide[:, rest:lanes], spare, 1)], axis=1)
        grad_down[...] = pltpu.roll(whole, spare, 1)[:, 0:ff].astype(BF16)[None]

    with jax.named_scope("drain"):
        exchanged(0, snd1, rcv1).wait_send()
        exchanged(1, snd2, rcv2).wait_send()
        exchanged(2, snd3, rcv3).wait_send()
        for n, ref in enumerate((ow_all, totals, hid_rcv, out_rcv)):
            pushed(n, ref).wait_send()
        for n, ref in enumerate((piece_rcv, out_piece, whole_piece)):
            got(n, ref).wait_send()
        ring_drain(weight_chains + head_chains + pooled_chains)
        twins(head_chains, lambda copy: copy.wait_send())
        for own, ring, to_right, steps, sem, slot, rows in down_chains + up_chains:
            place = ring.at[slot, pl.ds(0, steps), rows]
            remote(place, place, ring_send.at[sem], ring_recv.at[sem, 0], "dp", right).wait_send()


def hand_out(*refs):
    for src, dst in zip(refs[:5], refs[5:]):
        dst[...] = src[...]


def local(
    tokens,
    route_ids,
    route_weights,
    up_weight,
    down_weight,
    head_weight,
    out_weight,
    pool_ids,
    list_ids,
    clicks,
    ranks,
    alpha_table,
    beta_table,
):
    n_dp = lax.axis_size("dp")
    n_exp = lax.axis_size("expert")
    toks, width = tokens.shape
    ff = up_weight.shape[2]
    lanes = -(-ff // 128) * 128
    rest = 2 * ff - lanes
    units = head_weight.shape[0]
    cands = list_ids.shape[1]
    slots = n_exp * (MAIN + OVER)
    wire = pltpu.VMEM((n_exp, MAIN, width + width // 2), BF16)
    steps = n_dp // 2
    pairs = units * n_dp // 128
    vmem = pl.BlockSpec(memory_space=pltpu.VMEM)
    outs = pl.pallas_call(
        functools.partial(kernel, n_dp, n_exp),
        out_shape=(
            jax.ShapeDtypeStruct(up_weight.shape, BF16),
            jax.ShapeDtypeStruct(down_weight.shape, BF16),
            jax.ShapeDtypeStruct(head_weight.shape, F32),
            jax.ShapeDtypeStruct((1, units), F32),
            jax.ShapeDtypeStruct((1, 1), F32),
        ),
        in_specs=[vmem] * 13,
        out_specs=(vmem,) * 5,
        scratch_shapes=[
            wire,
            wire,
            wire,
            wire,
            wire,
            wire,
            pltpu.VMEM((n_exp * MAIN, toks), BF16),
            pltpu.VMEM((n_exp * OVER, toks), BF16),
            pltpu.VMEM((n_exp * MAIN, 2 * toks), BF16),
            pltpu.VMEM((n_exp * OVER, 2 * toks), BF16),
            pltpu.VMEM((2 * toks, n_exp * MAIN), BF16),
            pltpu.VMEM((2 * toks, n_exp * OVER), BF16),
            pltpu.VMEM((slots, width), BF16),
            pltpu.VMEM((slots, width), BF16),
            pltpu.VMEM((slots, lanes), F32),
            pltpu.VMEM((slots, lanes), BF16),
            pltpu.VMEM((slots, lanes), BF16),
            pltpu.VMEM((n_dp, width // n_dp, lanes), BF16),
            pltpu.VMEM((n_dp, width // n_dp, rest), BF16),
            pltpu.VMEM((width, lanes), BF16),
            pltpu.VMEM((n_dp, units, width), BF16),
            pltpu.VMEM((n_dp, 8, 128), F32),
            pltpu.VMEM((n_dp, width // n_dp, lanes), BF16),
            pltpu.VMEM((n_dp, width // n_dp, rest), BF16),
            pltpu.VMEM((2, steps, width // n_dp, lanes), BF16),
            pltpu.VMEM((2, steps, width // n_dp, rest), BF16),
            pltpu.VMEM((n_dp, 8, 128), F32),
            pltpu.VMEM((pairs, cands, 128), BF16),
            pltpu.VMEM((n_dp, cands, 128), BF16),
            pltpu.VMEM((n_dp, cands, width), BF16),
            pltpu.VMEM((pairs, 8, 128), F32),
            pltpu.VMEM((n_dp, 8, 128), F32),
            pltpu.VMEM((128, width), F32),
            pltpu.VMEM((n_exp, 16, 128), BF16),
            pltpu.VMEM((n_exp, 16, 128), BF16),
            pltpu.VMEM((n_exp, 16, 128), F32),
            pltpu.VMEM((n_exp, 8, 128), F32),
            pltpu.SemaphoreType.DMA((3,)),
            pltpu.SemaphoreType.DMA((3,)),
            pltpu.SemaphoreType.DMA((22,)),
            pltpu.SemaphoreType.DMA((22, steps)),
            pltpu.SemaphoreType.DMA((4,)),
            pltpu.SemaphoreType.DMA((4,)),
            pltpu.SemaphoreType.DMA((3,)),
            pltpu.SemaphoreType.DMA((3,)),
            pltpu.SemaphoreType.DMA((4,)),
            pltpu.SemaphoreType.DMA((4,)),
        ],
        compiler_params=pltpu.CompilerParams(
            collective_id=0, has_side_effects=True, vmem_limit_bytes=56 * 1024 * 1024
        ),
    )(
        tokens,
        route_ids.T,
        route_weights.T,
        up_weight,
        down_weight,
        head_weight,
        out_weight.reshape(1, units),
        pool_ids,
        list_ids,
        clicks,
        ranks,
        alpha_table.reshape(1, RANKS),
        beta_table.reshape(1, RANKS),
    )
    grad_up, grad_down, grad_head, grad_out, list_loss = pl.pallas_call(
        hand_out,
        out_shape=[jax.ShapeDtypeStruct(o.shape, o.dtype) for o in outs],
        in_specs=[vmem] * 5,
        out_specs=[vmem] * 5,
    )(*outs)
    return grad_up, grad_down, grad_head, grad_out.reshape(units), list_loss.reshape(1)


def solution(mesh):
    return jax.shard_map(
        local,
        mesh=mesh,
        in_specs=(
            P(("dp", "expert"), None),
            P(("dp", "expert"), None),
            P(("dp", "expert"), None),
            P("expert", "dp", None),
            P("expert", "dp", None),
            P("dp", None),
            P("dp"),
            P(("dp", "expert"), None),
            P(("dp", "expert"), None),
            P(("dp", "expert"), None),
            P(("dp", "expert"), None),
            P(),
            P(),
        ),
        out_specs=(
            P("expert", "dp", None),
            P("expert", "dp", None),
            P("dp", None),
            P("dp"),
            P("expert"),
        ),
        check_vma=False,
    )
```

```python
import functools

import jax
import jax.numpy as jnp
from jax import lax
from jax.experimental import pallas as pl
from jax.experimental.pallas import tpu as pltpu
from jax.sharding import PartitionSpec as P

LISTS = 8
RANKS = 32
MAIN = 16
OVER = 8
F32 = jnp.float32
BF16 = jnp.bfloat16
MESH = pl.DeviceIdType.MESH


def dot(a, b, ca=1, cb=0):
    return lax.dot_general(a, b, (((ca,), (cb,)), ((), ())), preferred_element_type=F32)


def iota(shape, dim):
    return lax.broadcasted_iota(jnp.int32, shape, dim)


def column(row, size):
    diagonal = iota((size, size), 0) == iota((size, size), 1)
    return jnp.sum(jnp.where(diagonal, jnp.broadcast_to(row, (size, size)), 0.0), axis=1, keepdims=True)


def split(value):
    high = value.astype(BF16)
    return high, (value - high.astype(F32)).astype(BF16)


def kernel(
    n_dp,
    n_exp,
    tok,
    ids,
    wts,
    up,
    down,
    head,
    out_w,
    pool,
    lists,
    clicks,
    ranks,
    alpha,
    beta,
    grad_up,
    grad_down,
    grad_head,
    grad_out,
    loss,
    snd1,
    rcv1,
    snd2,
    rcv2,
    snd3,
    rcv3,
    hot_main,
    hot_over,
    mix_main,
    mix_over,
    mix_main_t,
    mix_over_t,
    x_all,
    g_all,
    pre,
    act,
    pre_grad,
    wide_all,
    rest_all,
    down_full,
    head_all,
    ow_all,
    up_sum,
    down_sum,
    up_ring,
    down_ring,
    totals,
    hid_snd,
    hid_rcv,
    pooled_all,
    out_snd,
    out_rcv,
    head_term,
    piece_snd,
    piece_rcv,
    whole_piece,
    out_piece,
    a2a_send,
    a2a_recv,
    ring_send,
    ring_recv,
    dp_send,
    dp_recv,
    exp_send,
    exp_recv,
    twin_send,
    twin_recv,
):
    toks, width = tok.shape
    top = ids.shape[0]
    ff = up.shape[2]
    lanes = wide_all.shape[2]
    spare = lanes - ff
    rest = rest_all.shape[2]
    half = width // 2
    cands = lists.shape[1]
    units = head.shape[0]
    hidden = units * n_dp
    group = min(16, n_exp)
    groups = n_exp // group
    g_main, g_over = group * MAIN, group * OVER
    g_rows = g_main + g_over
    me_d = lax.axis_index("dp")
    me_e = lax.axis_index("expert")
    right = lax.rem(me_d + 1, n_dp)
    left = lax.rem(me_d + n_dp - 1, n_dp)

    def expert_peers(do):
        def body(k, carry):
            do(lax.rem(me_e + k, n_exp))
            return carry

        lax.fori_loop(1, n_exp, body, 0)

    def dp_peers(do):
        def body(k, carry):
            away = n_dp // 2 + ((k + 1) // 2) * (1 - 2 * lax.rem(k, 2))
            do(lax.rem(me_d + away, n_dp))
            return carry

        lax.fori_loop(0, n_dp - 1, body, 0)

    def remote(src, dst, send, recv, axis, peer):
        return pltpu.make_async_remote_copy(
            src_ref=src,
            dst_ref=dst,
            send_sem=send,
            recv_sem=recv,
            device_id={axis: peer},
            device_id_type=MESH,
        )

    def exchange(n, src, dst, p):
        return remote(src.at[p], dst.at[me_e], a2a_send.at[n], a2a_recv.at[n], "expert", p)

    next_e = lax.rem(me_e + 1, n_exp)

    def exchanged(n, src, dst):
        peers = pl.ds(0, n_exp - 1)
        return remote(src.at[peers], dst.at[peers], a2a_send.at[n], a2a_recv.at[n], "expert", next_e)

    def send_group(n, src, dst, g):
        def body(k, carry):
            p = g * group + lax.rem(me_e + k, group)

            @pl.when(p != me_e)
            def _():
                exchange(n, src, dst, p).start()

            return carry

        lax.fori_loop(0, group, body, 0)

    def keep_own(src, dst):
        dst[pl.ds(me_e, 1)] = src[pl.ds(me_e, 1)]

    def pack(dst, g, main, over):
        peers = pl.ds(g * group, group)
        dst[peers, :, 0:width] = main.astype(BF16).reshape(group, MAIN, width)
        low = over[:, 0:half].reshape(group, OVER, half)
        high = over[:, half:width].reshape(group, OVER, half)
        dst[peers, :, width : width + half] = jnp.concatenate([low, high], axis=1).astype(BF16)

    def unpack(src, g):
        peers = pl.ds(g * group, group)
        main = src[peers, :, 0:width].reshape(g_main, width)
        both = src[peers, :, width : width + half].astype(F32)
        low = both[:, 0:OVER, :].reshape(g_over, half)
        high = both[:, OVER : 2 * OVER, :].reshape(g_over, half)
        return main, jnp.concatenate([low, high], axis=1).astype(BF16)

    with jax.named_scope("greet"):
        barrier = pltpu.get_barrier_semaphore()
        expert_peers(
            lambda p: pl.semaphore_signal(barrier, inc=1, device_id={"expert": p}, device_id_type=MESH)
        )
        dp_peers(lambda p: pl.semaphore_signal(barrier, inc=1, device_id={"dp": p}, device_id_type=MESH))

    with jax.named_scope("slots"):
        pad = jnp.zeros((up.shape[1], spare), F32)
        turned = pltpu.roll(jnp.concatenate([down[0].astype(F32), pad], axis=1), lanes - spare, 1)
        up_wide = jnp.concatenate([up[0].astype(F32), pad], axis=1)
        own_wide = jnp.where(iota((up.shape[1], lanes), 1) < ff, up_wide, turned)
        wide_all[pl.ds(me_d, 1)] = own_wide.astype(BF16)[None]
        rest_all[pl.ds(me_d, 1)] = turned[:, 0:rest].astype(BF16)[None]
        head_all[pl.ds(me_d, 1)] = head[...].reshape(1, units, width)
        expert = iota((n_exp, toks), 0)
        named_t = jnp.zeros((n_exp, toks), F32)
        weight_t = jnp.zeros((n_exp, toks), F32)
        for k in range(top):
            hit = ids[k : k + 1, :] == expert
            named_t = jnp.where(hit, 1.0, named_t)
            weight_t = jnp.where(hit, wts[k : k + 1, :], weight_t)
        earlier = jnp.where(iota((toks, toks), 0) < iota((toks, toks), 1), 1.0, 0.0).astype(BF16)
        slot_t = jnp.where(named_t > 0.5, dot(named_t.astype(BF16), earlier), -1.0)

        def one_hot(first, rows):
            slot = (iota((n_exp, rows, toks), 1) + first).astype(F32)
            return jnp.where(slot_t[:, None, :] == slot, 1.0, 0.0).reshape(n_exp * rows, toks)

        hot_main[...] = one_hot(0, MAIN).astype(BF16)
        hot_over[...] = one_hot(MAIN, OVER).astype(BF16)

        def dispatch(g, carry):
            pack(
                snd1,
                g,
                dot(hot_main[pl.ds(g * g_main, g_main), :], tok[...]),
                dot(hot_over[pl.ds(g * g_over, g_over), :], tok[...]),
            )
            return carry

        lax.fori_loop(0, groups, dispatch, 0)
        parity = lax.rem(me_d, 2)
        own_row = jnp.concatenate([out_w[...], jnp.zeros((1, 128 - units), F32)], axis=1)
        own_row = jnp.where(parity == 0, own_row, pltpu.roll(own_row, units, 1))
        ow_all[pl.ds(me_d, 1)] = jnp.broadcast_to(own_row, (8, 128))[None]
        keep_own(snd1, rcv1)

    with jax.named_scope("barrier_wait"):
        pl.semaphore_wait(barrier, n_exp - 1 + n_dp - 1)

    far = n_dp // 2
    near = n_dp - 1 - far

    def hop(chain, step):
        buf, rows, to_right, steps, sem = chain
        owner = lax.rem(me_d + (n_dp - step if to_right else step), n_dp)
        place = buf.at[owner, rows]
        return remote(
            place, place, ring_send.at[sem], ring_recv.at[sem, step], "dp", right if to_right else left
        )

    def came(chain, step):
        buf, rows, to_right, steps, sem = chain
        owner = lax.rem(me_d + (n_dp - 1 - step if to_right else step + 1), n_dp)
        place = buf.at[owner, rows]
        remote(
            place, place, ring_send.at[sem], ring_recv.at[sem, step], "dp", right if to_right else left
        ).wait_recv()

    def ring_start(chains):
        for chain in chains:
            hop(chain, 0).start()

    def ring_step(chains, step, each):
        for chain in chains:
            steps = chain[3]

            @pl.when(step < steps)
            def _(chain=chain, steps=steps):
                came(chain, step)

                @pl.when(step + 1 < steps)
                def _():
                    hop(chain, step + 1).start()

                if each is not None:
                    each(chain, step).start()

    def ring_steps(chains, first, last, each=None):
        def body(step, carry):
            ring_step(chains, step, each)
            return carry

        if first < last:
            lax.fori_loop(first, last, body, 0)

    def ring_drain(chains):
        for buf, rows, to_right, steps, sem in chains:
            place = buf.at[pl.ds(0, steps), rows]
            remote(place, place, ring_send.at[sem], ring_recv.at[sem, 0], "dp", right).wait_send()

    upper = pl.ds(0, units // 2)
    lower = pl.ds(units // 2, units // 2)
    weight_chains = [
        (wide_all, upper, True, far, 0),
        (wide_all, upper, False, near, 1),
        (wide_all, lower, True, near, 2),
        (wide_all, lower, False, far, 3),
        (rest_all, upper, True, far, 4),
        (rest_all, upper, False, near, 5),
        (rest_all, lower, True, near, 6),
        (rest_all, lower, False, far, 7),
    ]
    core = lax.rem(me_e, 2)
    twin = me_e + 1 - 2 * core
    quarter = units // 4

    def head_rows(side, part):
        return pl.ds(pl.multiple_of(side * 2 * quarter + part * quarter, 16), quarter)

    def head_half(side):
        return [
            (head_all, head_rows(side, 0), True, far, 8),
            (head_all, head_rows(side, 0), False, near, 9),
            (head_all, head_rows(side, 1), True, near, 10),
            (head_all, head_rows(side, 1), False, far, 11),
        ]

    head_chains = head_half(core)

    def hand_over(chain, step):
        buf, rows, to_right, steps, sem = chain
        owner = lax.rem(me_d + (n_dp - 1 - step if to_right else step + 1), n_dp)
        place = buf.at[owner, rows]
        return remote(place, place, twin_send.at[sem - 8], twin_recv.at[sem - 8], "expert", twin)

    def twins(chains, do):
        for buf, rows, to_right, steps, sem in chains:
            place = buf.at[pl.ds(0, steps), rows]
            do(remote(place, place, twin_send.at[sem - 8], twin_recv.at[sem - 8], "expert", twin))

    pooled_chains = [
        (pooled_all, pl.ds(0, cands), True, far, 20),
        (pooled_all, pl.ds(0, cands), False, near, 21),
    ]

    def push(n, src, dst, p):
        return remote(src, dst.at[me_d], dp_send.at[n], dp_recv.at[n], "dp", p)

    def pushed(n, dst):
        peers = pl.ds(0, n_dp - 1)
        return remote(dst.at[peers], dst.at[peers], dp_send.at[n], dp_recv.at[n], "dp", right)

    with jax.named_scope("dispatch_send"):
        ring_start(weight_chains)
        for g in range(groups):
            send_group(0, snd1, rcv1, g)
        dp_peers(lambda p: push(0, ow_all.at[me_d], ow_all, p).start())

    with jax.named_scope("mix_tables"):
        weight_high, weight_low = split(weight_t)

        def spread(part, hot, rows):
            wide = jnp.broadcast_to(part.astype(F32)[:, None, :], (n_exp, rows, toks))
            return hot[...].astype(F32) * wide.reshape(n_exp * rows, toks)

        def both(hot, rows):
            return jnp.concatenate(
                [spread(weight_high, hot, rows), spread(weight_low, hot, rows)], axis=1
            )

        table = both(hot_main, MAIN)
        mix_main[...] = table.astype(BF16)
        mix_main_t[...] = jnp.transpose(table).astype(BF16)
        table = both(hot_over, OVER)
        mix_over[...] = table.astype(BF16)
        mix_over_t[...] = jnp.transpose(table).astype(BF16)

    with jax.named_scope("weight_ring"):
        head_at = max(0, min(3, far - 1))
        ring_steps(weight_chains, 0, far - 1 - head_at)
        ring_start(head_chains)
        ring_steps(weight_chains, far - 1 - head_at, far - head_at)

        def both_steps(k, carry):
            ring_step(weight_chains, k + (far - head_at), None)
            ring_step(head_chains, k, hand_over)
            return carry

        lax.fori_loop(0, head_at, both_steps, 0)

    with jax.named_scope("dispatch_wait"):
        exchanged(0, snd1, rcv1).wait_recv()

    with jax.named_scope("expert_forward"):
        if head_at < far:
            ring_step(head_chains, head_at, hand_over)
            head_at += 1
        down_full[:, 0:rest] = rest_all[...].reshape(width, rest)
        down_full[:, rest:lanes] = wide_all[:, :, rest:lanes].reshape(width, lanes - rest)

        def no_column(rows):
            lane = iota((rows, lanes), 1)
            return (lane >= rest) & (lane < rest + spare)

        def forward(g):
            main, over = unpack(rcv1, g)
            rows = pl.ds(g * g_rows, g_rows)
            x = jnp.concatenate([main, over], axis=0)
            x_all[rows, :] = x
            natural = dot(x, wide_all[...].reshape(width, lanes))
            pre_act = jnp.where(no_column(g_rows), 0.0, pltpu.roll(natural, lanes - spare, 1))
            pre[rows, :] = pre_act
            activated = (pre_act * jax.nn.sigmoid(pre_act)).astype(BF16)
            act[rows, :] = activated
            out = dot(activated, down_full[...], 1, 1)
            pack(snd2, g, out[0:g_main], out[g_main:g_rows])
            send_group(1, snd2, rcv2, g)

        for g in range(groups):
            forward(g)
            if head_at < far:
                ring_step(head_chains, head_at, hand_over)
                head_at += 1
        keep_own(snd2, rcv2)

    with jax.named_scope("head_ring"):
        ring_steps(head_chains, head_at, far, hand_over)
        twins(head_half(1 - core), lambda copy: copy.wait_recv())

    with jax.named_scope("slope"):

        def slope(g, carry):
            rows = pl.ds(pl.multiple_of(g * (g_rows // 4), 16), g_rows // 4)
            pre_act = pre[rows, :]
            sigmoid = jax.nn.sigmoid(pre_act)
            slope_of = sigmoid * (1.0 + pre_act * (1.0 - sigmoid))
            pre[rows, :] = jnp.where(no_column(g_rows // 4), 0.0, slope_of)
            return carry

        lax.fori_loop(0, groups * 4, slope, 0)
        pool_row = pool[...].astype(F32)
        member_t = jnp.where(iota((cands, toks), 0).astype(F32) == pool_row, 1.0, 0.0)
        counts = jnp.sum(member_t, axis=1, keepdims=True)
        pool_column = column(pool_row, toks)
        member = jnp.where(iota((toks, cands), 1).astype(F32) == pool_column, 1.0, 0.0).astype(BF16)
        member_t = member_t.astype(BF16)
        list_hot = jnp.where(
            iota((cands, 128), 1).astype(F32) == column(lists[...].astype(F32), cands), 1.0, 0.0
        )
        rank_hot = jnp.where(
            iota((cands, RANKS), 1).astype(F32) == column(ranks[...].astype(F32), cands), 1.0, 0.0
        )
        alpha_of = jnp.sum(rank_hot * alpha[...], axis=1, keepdims=True)
        beta_of = jnp.sum(rank_hot * beta[...], axis=1, keepdims=True)
        corrected = (column(clicks[...].astype(F32), cands) - beta_of) / alpha_of
        pushed(0, ow_all).wait_recv()
        ow_row = jnp.concatenate(
            [(ow_all[2 * k] + ow_all[2 * k + 1])[0:1] for k in range(hidden // 128)], axis=1
        )

    with jax.named_scope("return_wait"):
        exchanged(1, snd2, rcv2).wait_recv()

    with jax.named_scope("mix"):
        stacked = jnp.zeros((2 * toks, width), F32)
        for g in range(groups):
            main, over = unpack(rcv2, g)
            stacked = stacked + dot(mix_main_t[:, g * g_main : (g + 1) * g_main], main)
            stacked = stacked + dot(mix_over_t[:, g * g_over : (g + 1) * g_over], over)
        mixed = tok[...].astype(F32) + (stacked[0:toks] + stacked[toks : 2 * toks])
        inv_rms = lax.rsqrt(jnp.mean(mixed * mixed, axis=1, keepdims=True) + 1e-06)
        normed = mixed * inv_rms
        normed_high, normed_low = split(normed)
        pooled_sum = dot(member_t, normed_high) + dot(member_t, normed_low)
        pooled = (pooled_sum / counts).astype(BF16)
        pooled_all[pl.ds(me_d, 1)] = pooled.reshape(1, cands, width)
        ring_start(pooled_chains)
    with jax.named_scope("head_forward"):
        head_act = jnp.tanh(dot(pooled, head_all[...].reshape(hidden, width), 1, 1))
        scores = jnp.sum(head_act * ow_row, axis=1, keepdims=True)
        exp_scores = jnp.exp(scores)
        tile_row = iota((8, 128), 0)
        terms = jnp.zeros((8, 128), F32)
        for k, value in enumerate((exp_scores, corrected, corrected * scores)):
            terms = jnp.where(tile_row == k, jnp.sum(value * list_hot, axis=0, keepdims=True), terms)
        totals[pl.ds(me_d, 1)] = terms.reshape(1, 8, 128)
    with jax.named_scope("totals"):
        dp_peers(lambda p: push(1, totals.at[me_d], totals, p).start())
        pooled_at = min(2, far)
        ring_steps(pooled_chains, 0, pooled_at)
        pushed(1, totals).wait_recv()
    with jax.named_scope("head_backward"):
        total = jnp.sum(totals[...], axis=0)
        in_list = iota((1, 128), 1) < LISTS
        exp_total = jnp.where(in_list, total[0:1], 1.0)
        click_total = jnp.where(in_list, total[1:2], 0.0)
        cross_total = jnp.where(in_list, total[2:3], 0.0)
        loss[...] = jnp.sum(click_total * jnp.log(exp_total) - cross_total, axis=1, keepdims=True)
        ratio = jnp.sum(list_hot * (click_total / exp_total), axis=1, keepdims=True)
        cand_grad = ratio * exp_scores - corrected
        hid_grad = (cand_grad * ow_row * (1.0 - head_act * head_act)).astype(BF16)
        pooled_grad = dot(hid_grad, head_all[...].reshape(hidden, width)) / counts
        grad_high, grad_low = split(pooled_grad)
        normed_grad = dot(member, grad_high) + dot(member, grad_low)
        mixed_grad = inv_rms * (normed_grad - normed * jnp.mean(normed_grad * normed, axis=1, keepdims=True))
        once = mixed_grad.astype(BF16)
        twice = jnp.concatenate([once, once], axis=0)
    with jax.named_scope("grad_send"):
        for g in range(groups):
            pack(
                snd3,
                g,
                dot(mix_main[g * g_main : (g + 1) * g_main, :], twice),
                dot(mix_over[g * g_over : (g + 1) * g_over, :], twice),
            )
            send_group(2, snd3, rcv3, g)
        keep_own(snd3, rcv3)

        out_term = jnp.sum(cand_grad * head_act, axis=0, keepdims=True)
        for k in range(hidden // 128):
            hid_snd[k] = hid_grad[:, k * 128 : (k + 1) * 128]
            out_snd[k] = jnp.broadcast_to(out_term[:, k * 128 : (k + 1) * 128], (8, 128))
        hid_rcv[pl.ds(me_d, 1)] = hid_snd[pl.ds(me_d // 2, 1)]
        out_rcv[pl.ds(me_d, 1)] = out_snd[pl.ds(me_d // 2, 1)]

        def send_terms(p):
            push(2, hid_snd.at[p // 2], hid_rcv, p).start()
            push(3, out_snd.at[p // 2], out_rcv, p).start()

        dp_peers(send_terms)

    with jax.named_scope("pooled_ring"):
        ring_steps(pooled_chains, pooled_at, far)

    with jax.named_scope("grad_wait"):
        exchanged(2, snd3, rcv3).wait_recv()

    tile = min(1024, width)
    blocks = tile // units

    def down_part(f, carry):
        part = dot(g_all[:, pl.ds(pl.multiple_of(f * tile, 128), tile)], act[...], 0, 0)
        place = pl.ds(f * blocks, blocks)
        down_sum[place] = part[:, 0:rest].astype(BF16).reshape(blocks, units, rest)
        up_sum[place, :, rest:lanes] = part[:, rest:lanes].astype(BF16).reshape(blocks, units, lanes - rest)
        return carry

    def up_part(f, carry):
        part = dot(x_all[:, pl.ds(pl.multiple_of(f * tile, 128), tile)], pre_grad[...], 0, 0)
        place = pl.ds(f * blocks, blocks)
        up_sum[place, :, 0:rest] = part[:, 0:rest].astype(BF16).reshape(blocks, units, rest)
        below = up_sum[place, :, rest:lanes].astype(F32).reshape(tile, lanes - rest)
        last = jnp.where(iota(below.shape, 1) < spare, pltpu.roll(below, spare, 1), part[:, rest:lanes])
        up_sum[place, :, rest:lanes] = last.astype(BF16).reshape(blocks, units, lanes - rest)
        return carry

    def sum_hop(chain, step):
        own, ring, to_right, steps, sem, slot, rows = chain
        if isinstance(step, int) and step == 0:
            owner = lax.rem(me_d + (steps if to_right else n_dp - steps), n_dp)
            src = own.at[owner, rows]
        else:
            src = ring.at[slot, step - 1, rows]
        return remote(
            src,
            ring.at[slot, step, rows],
            ring_send.at[sem],
            ring_recv.at[sem, step],
            "dp",
            right if to_right else left,
        )

    def sum_came(chain, step):
        own, ring, to_right, steps, sem, slot, rows = chain
        place = ring.at[slot, step, rows]
        remote(
            place, place, ring_send.at[sem], ring_recv.at[sem, step], "dp", right if to_right else left
        ).wait_recv()

    def sum_chains(own, ring, sem):
        return [
            (own, ring, True, far, sem, 0, upper),
            (own, ring, False, near, sem + 1, 1, upper),
            (own, ring, True, near, sem + 2, 0, lower),
            (own, ring, False, far, sem + 3, 1, lower),
        ]

    up_chains = sum_chains(up_sum, up_ring, 12)
    down_chains = sum_chains(down_sum, down_ring, 16)

    with jax.named_scope("down_term"):

        def gather(g, carry):
            main, over = unpack(rcv3, g)
            rows = pl.ds(pl.multiple_of(g * g_rows, 16), g_rows)
            g_all[rows, :] = jnp.concatenate([main, over], axis=0)
            return carry

        lax.fori_loop(0, groups, gather, 0)
        lax.fori_loop(0, width // tile, down_part, 0)
        for chain in down_chains:
            sum_hop(chain, 0).start()

    with jax.named_scope("up_term"):

        pre_grad[...] = (dot(g_all[...], down_full[...]) * pre[...]).astype(BF16)
        lax.fori_loop(0, width // tile, up_part, 0)
        for chain in up_chains:
            sum_hop(chain, 0).start()

    columns = width // 128
    with jax.named_scope("head_term"):

        pushed(2, hid_rcv).wait_recv()
        pushed(3, out_rcv).wait_recv()
        head_term[...] = dot(
            hid_rcv[...].reshape(n_dp * cands, 128), pooled_all[...].reshape(n_dp * cands, width), 0, 0
        )
        mine = head_term[pl.ds(pl.multiple_of(parity * units, 8), units), :].astype(BF16)
        for q in range(n_exp):
            a, b = q // columns, q % columns
            piece_snd[q] = mine[a * 16 : (a + 1) * 16, b * 128 : (b + 1) * 128]
        piece_rcv[pl.ds(me_e, 1)] = piece_snd[pl.ds(me_e, 1)]
        out_piece[pl.ds(me_e, 1)] = jnp.sum(out_rcv[...], axis=0).reshape(1, 8, 128)

    def piece(p):
        return remote(piece_snd.at[p], piece_rcv.at[me_e], exp_send.at[0], exp_recv.at[0], "expert", p)

    def out_push(p):
        return remote(out_piece.at[me_e], out_piece.at[me_e], exp_send.at[1], exp_recv.at[1], "expert", p)

    def whole_push(p):
        return remote(whole_piece.at[me_e], whole_piece.at[me_e], exp_send.at[2], exp_recv.at[2], "expert", p)

    def got(n, ref):
        peers = pl.ds(0, n_exp - 1)
        return remote(ref.at[peers], ref.at[peers], exp_send.at[n], exp_recv.at[n], "expert", next_e)

    def send_pieces(p):
        piece(p).start()
        out_push(p).start()

    expert_peers(send_pieces)

    def sum_steps(first, last):
        def body(step, carry):
            for chain in down_chains + up_chains:
                steps = chain[3]

                @pl.when(step + 1 < steps)
                def _(chain=chain):
                    own, ring, to_right, steps, sem, slot, rows = chain
                    sum_came(chain, step)
                    owner = lax.rem(
                        me_d + (steps - 1 - step if to_right else n_dp - (steps - 1) + step), n_dp
                    )
                    total = ring[slot, pl.ds(step, 1), rows].astype(F32) + own[pl.ds(owner, 1), rows].astype(F32)
                    ring[slot, pl.ds(step, 1), rows] = total.astype(BF16)
                    sum_hop(chain, step + 1).start()

            return carry

        lax.fori_loop(first, last, body, 0)

    with jax.named_scope("sum_ring_first"):
        middle = min(3, far - 1)
        sum_steps(0, middle)

    with jax.named_scope("head_pieces"):
        got(0, piece_rcv).wait_recv()
        whole_piece[pl.ds(me_e, 1)] = jnp.sum(piece_rcv[...].astype(F32), axis=0).reshape(1, 16, 128)
        expert_peers(lambda p: whole_push(p).start())

    with jax.named_scope("sum_ring_last"):
        sum_steps(middle, far - 1)

    with jax.named_scope("head_out"):
        got(1, out_piece).wait_recv()
        out_all = jnp.sum(out_piece[...], axis=0)[0:1]
        out_pair = jnp.where(parity == 0, out_all, pltpu.roll(out_all, 128 - units, 1))
        grad_out[...] = out_pair[:, 0:units]
        got(2, whole_piece).wait_recv()
        for q in range(n_exp):
            a, b = q // columns, q % columns
            grad_head[a * 16 : (a + 1) * 16, b * 128 : (b + 1) * 128] = whole_piece[q]

    with jax.named_scope("sum_end"):
        sums = []
        for chains in (down_chains, up_chains):
            halves = []
            for pair in (chains[0:2], chains[2:4]):
                total = 0.0
                for chain in pair:
                    own, ring, to_right, steps, sem, slot, rows = chain
                    sum_came(chain, steps - 1)
                    total = total + ring[slot, steps - 1, rows].astype(F32)
                halves.append(total + own[pl.ds(me_d, 1), rows][0].astype(F32))
            sums.append(jnp.concatenate(halves, axis=0))
        most, wide = sums
        grad_up[...] = pltpu.roll(wide, spare, 1)[:, 0:ff].astype(BF16)[None]
        whole = jnp.concatenate([most, pltpu.roll(wide[:, rest:lanes], spare, 1)], axis=1)
        grad_down[...] = pltpu.roll(whole, spare, 1)[:, 0:ff].astype(BF16)[None]

    with jax.named_scope("drain"):
        exchanged(0, snd1, rcv1).wait_send()
        exchanged(1, snd2, rcv2).wait_send()
        exchanged(2, snd3, rcv3).wait_send()
        for n, ref in enumerate((ow_all, totals, hid_rcv, out_rcv)):
            pushed(n, ref).wait_send()
        for n, ref in enumerate((piece_rcv, out_piece, whole_piece)):
            got(n, ref).wait_send()
        ring_drain(weight_chains + head_chains + pooled_chains)
        twins(head_chains, lambda copy: copy.wait_send())
        for own, ring, to_right, steps, sem, slot, rows in down_chains + up_chains:
            place = ring.at[slot, pl.ds(0, steps), rows]
            remote(place, place, ring_send.at[sem], ring_recv.at[sem, 0], "dp", right).wait_send()


def hand_out(*refs):
    for src, dst in zip(refs[:5], refs[5:]):
        dst[...] = src[...]


def local(
    tokens,
    route_ids,
    route_weights,
    up_weight,
    down_weight,
    head_weight,
    out_weight,
    pool_ids,
    list_ids,
    clicks,
    ranks,
    alpha_table,
    beta_table,
):
    n_dp = lax.axis_size("dp")
    n_exp = lax.axis_size("expert")
    toks, width = tokens.shape
    ff = up_weight.shape[2]
    lanes = -(-ff // 128) * 128
    rest = 2 * ff - lanes
    units = head_weight.shape[0]
    cands = list_ids.shape[1]
    slots = n_exp * (MAIN + OVER)
    wire = pltpu.VMEM((n_exp, MAIN, width + width // 2), BF16)
    steps = n_dp // 2
    pairs = units * n_dp // 128
    vmem = pl.BlockSpec(memory_space=pltpu.VMEM)
    outs = pl.pallas_call(
        functools.partial(kernel, n_dp, n_exp),
        out_shape=(
            jax.ShapeDtypeStruct(up_weight.shape, BF16),
            jax.ShapeDtypeStruct(down_weight.shape, BF16),
            jax.ShapeDtypeStruct(head_weight.shape, F32),
            jax.ShapeDtypeStruct((1, units), F32),
            jax.ShapeDtypeStruct((1, 1), F32),
        ),
        in_specs=[vmem] * 13,
        out_specs=(vmem,) * 5,
        scratch_shapes=[
            wire,
            wire,
            wire,
            wire,
            wire,
            wire,
            pltpu.VMEM((n_exp * MAIN, toks), BF16),
            pltpu.VMEM((n_exp * OVER, toks), BF16),
            pltpu.VMEM((n_exp * MAIN, 2 * toks), BF16),
            pltpu.VMEM((n_exp * OVER, 2 * toks), BF16),
            pltpu.VMEM((2 * toks, n_exp * MAIN), BF16),
            pltpu.VMEM((2 * toks, n_exp * OVER), BF16),
            pltpu.VMEM((slots, width), BF16),
            pltpu.VMEM((slots, width), BF16),
            pltpu.VMEM((slots, lanes), F32),
            pltpu.VMEM((slots, lanes), BF16),
            pltpu.VMEM((slots, lanes), BF16),
            pltpu.VMEM((n_dp, width // n_dp, lanes), BF16),
            pltpu.VMEM((n_dp, width // n_dp, rest), BF16),
            pltpu.VMEM((width, lanes), BF16),
            pltpu.VMEM((n_dp, units, width), BF16),
            pltpu.VMEM((n_dp, 8, 128), F32),
            pltpu.VMEM((n_dp, width // n_dp, lanes), BF16),
            pltpu.VMEM((n_dp, width // n_dp, rest), BF16),
            pltpu.VMEM((2, steps, width // n_dp, lanes), BF16),
            pltpu.VMEM((2, steps, width // n_dp, rest), BF16),
            pltpu.VMEM((n_dp, 8, 128), F32),
            pltpu.VMEM((pairs, cands, 128), BF16),
            pltpu.VMEM((n_dp, cands, 128), BF16),
            pltpu.VMEM((n_dp, cands, width), BF16),
            pltpu.VMEM((pairs, 8, 128), F32),
            pltpu.VMEM((n_dp, 8, 128), F32),
            pltpu.VMEM((128, width), F32),
            pltpu.VMEM((n_exp, 16, 128), BF16),
            pltpu.VMEM((n_exp, 16, 128), BF16),
            pltpu.VMEM((n_exp, 16, 128), F32),
            pltpu.VMEM((n_exp, 8, 128), F32),
            pltpu.SemaphoreType.DMA((3,)),
            pltpu.SemaphoreType.DMA((3,)),
            pltpu.SemaphoreType.DMA((22,)),
            pltpu.SemaphoreType.DMA((22, steps)),
            pltpu.SemaphoreType.DMA((4,)),
            pltpu.SemaphoreType.DMA((4,)),
            pltpu.SemaphoreType.DMA((3,)),
            pltpu.SemaphoreType.DMA((3,)),
            pltpu.SemaphoreType.DMA((4,)),
            pltpu.SemaphoreType.DMA((4,)),
        ],
        compiler_params=pltpu.CompilerParams(
            collective_id=0, has_side_effects=True, vmem_limit_bytes=56 * 1024 * 1024
        ),
    )(
        tokens,
        route_ids.T,
        route_weights.T,
        up_weight,
        down_weight,
        head_weight,
        out_weight.reshape(1, units),
        pool_ids,
        list_ids,
        clicks,
        ranks,
        alpha_table.reshape(1, RANKS),
        beta_table.reshape(1, RANKS),
    )
    grad_up, grad_down, grad_head, grad_out, list_loss = pl.pallas_call(
        hand_out,
        out_shape=[jax.ShapeDtypeStruct(o.shape, o.dtype) for o in outs],
        in_specs=[vmem] * 5,
        out_specs=[vmem] * 5,
    )(*outs)
    return grad_up, grad_down, grad_head, grad_out.reshape(units), list_loss.reshape(1)


def solution(mesh):
    return jax.shard_map(
        local,
        mesh=mesh,
        in_specs=(
            P(("dp", "expert"), None),
            P(("dp", "expert"), None),
            P(("dp", "expert"), None),
            P("expert", "dp", None),
            P("expert", "dp", None),
            P("dp", None),
            P("dp"),
            P(("dp", "expert"), None),
            P(("dp", "expert"), None),
            P(("dp", "expert"), None),
            P(("dp", "expert"), None),
            P(),
            P(),
        ),
        out_specs=(
            P("expert", "dp", None),
            P("expert", "dp", None),
            P("dp", None),
            P("dp"),
            P("expert"),
        ),
        check_vma=False,
    )
```
